128 devices in a mesh: by: 8 (over x_hi, z), bx: 16 (over x_lo, y, core).
Axes of the slice: x: 4 (x_hi: 2, x_lo: 2; x = x_hi * 2 + x_lo), y: 4, z: 4, core: 2. Of those that a mesh axis runs over, the one named last changes fastest.
Arguments:
- eastward_flow: float32 [62, 64, 4096], P(None, 'by', 'bx'), may hold values from -6 to 6
- northward_flow: float32 [62, 64, 4096], P(None, 'by', 'bx'), may hold values from -6 to 6
- heat_anomaly: float32 [62, 64, 4096], P(None, 'by', 'bx'), may hold values from -6 to 6
- salt_anomaly: float32 [62, 64, 4096], P(None, 'by', 'bx'), may hold values from -6 to 6
- air_stress_forcing: float32 [2, 64, 4096], P(None, 'by', 'bx'), may hold values from -6 to 6
- earlier_sea_height_load: float32 [64, 4096], P('by', 'bx'), may hold values from -6 to 6
- ocean_layer_depths: int32 [64, 4096], P('by', 'bx'), may hold values from 0 to 62, as said below
Outputs:
- east_new: float32 [62, 64, 4096], P(None, 'by', 'bx')
- north_new: float32 [62, 64, 4096], P(None, 'by', 'bx')
- temperature_new: float32 [62, 64, 4096], P(None, 'by', 'bx')
- salinity_new: float32 [62, 64, 4096], P(None, 'by', 'bx')
- surface_new: float32 [64, 4096], P('by', 'bx')
The draws below stay inside these ranges and needn't reach their ends.
Inputs may be any that keep to these rules, and one draw needn't show every extreme that they name: `ocean_layer_depths`: land (0) covers whole aligned tiles of 8 x 8 cells; every ocean column has 1 to 62 levels.
All inputs are finite; a program needn't handle non-finite values.
Results may differ from the reference program's by a relative error of at most 0.0003.
Values sent between devices are 32-bit elements; how exact they have to be, the bound alone decides.
A program may use at most 192 MiB of HBM per device.

```python
import math
import jax
import jax.numpy as jnp

DEPTH_LAYERS = 62
ITERS = 4
NORTHWARD_CELLS = 64
EASTWARD_CELLS = 4096


def draw_ocean_layer_depths(key, part):
    key = jax.random.fold_in(key, 7)
    tile_key, level_key = jax.random.split(key)
    tiles = jax.random.randint(tile_key, (NORTHWARD_CELLS // 8 + 1, EASTWARD_CELLS // 8 + 1), 0, 5)
    land_cells = tiles[jnp.arange(NORTHWARD_CELLS) // 8][:, jnp.arange(EASTWARD_CELLS) // 8] == 0
    depth = jax.random.randint(level_key, (NORTHWARD_CELLS, EASTWARD_CELLS), 1, DEPTH_LAYERS + 1)
    return jnp.where(land_cells, 0, depth).astype(jnp.int32)


def steps_of(key, dims, cuts, least, high):
    factor_of = 1.0
    for dim, parts in cuts:
        steps = jax.random.uniform(jax.random.fold_in(jax.random.fold_in(key, 6), dim), (parts,), jnp.float32, least / len(cuts), high / len(cuts))
        factor_of = factor_of * jnp.repeat(jnp.exp(steps), dims[dim] // parts).reshape((-1,) + (1,) * (len(dims) - 1 - dim))
    return factor_of


def bell_draw(key, shape, deviation, limit, cuts=(), held_as=jnp.bfloat16):
    values = deviation * jax.random.normal(key, shape, jnp.float32)
    if cuts:
        values = values * steps_of(key, shape, cuts, -0.22, 0.18)
    return jnp.clip(values, -limit, limit).astype(held_as)


def setup_inputs(seed: int = 0) -> dict:
    keys = jax.random.split(jax.random.key(seed), 8)
    eastward_flow = bell_draw(keys[0], (DEPTH_LAYERS, NORTHWARD_CELLS, EASTWARD_CELLS), 1.0, 6.0, ((1, 8), (2, 16)), jnp.float32)
    northward_flow = bell_draw(keys[1], (DEPTH_LAYERS, NORTHWARD_CELLS, EASTWARD_CELLS), 1.0, 6.0, ((1, 8), (2, 16)), jnp.float32)
    heat_anomaly = bell_draw(keys[2], (DEPTH_LAYERS, NORTHWARD_CELLS, EASTWARD_CELLS), 1.0, 6.0, ((1, 8), (2, 16)), jnp.float32)
    salt_anomaly = bell_draw(keys[3], (DEPTH_LAYERS, NORTHWARD_CELLS, EASTWARD_CELLS), 1.0, 6.0, ((1, 8), (2, 16)), jnp.float32)
    air_stress_forcing = bell_draw(keys[4], (2, NORTHWARD_CELLS, EASTWARD_CELLS), 1.0, 6.0, ((1, 8), (2, 16)), jnp.float32)
    earlier_sea_height_load = bell_draw(keys[5], (NORTHWARD_CELLS, EASTWARD_CELLS), 1.0, 6.0, ((0, 8), (1, 16)), jnp.float32)
    ocean_layer_depths = draw_ocean_layer_depths(jax.random.fold_in(keys[7], 71), 0)
    return {"eastward_flow": eastward_flow, "northward_flow": northward_flow, "heat_anomaly": heat_anomaly, "salt_anomaly": salt_anomaly, "air_stress_forcing": air_stress_forcing, "earlier_sea_height_load": earlier_sea_height_load, "ocean_layer_depths": ocean_layer_depths}


KAPPA = 0.004
ADVECT = 0.25
PRESS = 0.1
WIND = 0.5
PHI = 0.5
DIVERGE = 2.0
LOWER = 0.2
UPPER = 2.0


def chebyshev_weights(count):
    middle = 0.5 * (UPPER + LOWER)
    half_span = 0.5 * (UPPER - LOWER)
    ratio_value = middle / half_span
    rho_now = 1.0 / ratio_value
    updates = []
    for index in range(count - 1):
        rho_next = 1.0 / (2.0 * ratio_value - rho_now)
        updates.append((rho_next * rho_now, 2.0 * rho_next / half_span))
        rho_now = rho_next
    return 1.0 / middle, updates


def shrink(field, width):
    return field[..., width:field.shape[-2] - width, width:field.shape[-1] - width]


def sides(field):
    return (field[..., 1:-1, 1:-1], field[..., 1:-1, 2:], field[..., 1:-1, :-2],
            field[..., 2:, 1:-1], field[..., :-2, 1:-1])


def laplacian(field, mask):
    cell_here, cell_east, cell_west, cell_north, cell_south = sides(field)
    mask_here, mask_east, mask_west, mask_north, mask_south = sides(mask)
    return (mask_here * mask_east * (cell_east - cell_here) + mask_here * mask_west * (cell_west - cell_here)
            + mask_here * mask_north * (cell_north - cell_here) + mask_here * mask_south * (cell_south - cell_here))


def gradients(field, mask):
    cell_here, cell_east, cell_west, cell_north, cell_south = sides(field)
    mask_here, mask_east, mask_west, mask_north, mask_south = sides(mask)
    along_x = 0.5 * (mask_here * mask_east * (cell_east - cell_here) + mask_here * mask_west * (cell_here - cell_west))
    along_y = 0.5 * (mask_here * mask_north * (cell_north - cell_here) + mask_here * mask_south * (cell_here - cell_south))
    return along_x, along_y


def wet_levels(depth, levels):
    return jnp.where(jnp.arange(levels)[:, None, None] < depth[None], 1.0, 0.0).astype(jnp.float32)


def coriolis_rows(first_row, count, total_rows):
    rows_float = (first_row + jnp.arange(count)).astype(jnp.float32)
    return (1.2 * jnp.sin(0.9 * math.pi * ((rows_float + 0.5) / total_rows - 0.5)))[:, None]


def tendency(ocean_state_arrays, wind, wet, coriolis):
    east_vel, north_vel, temper, saline = ocean_state_arrays
    inner = shrink(wet, 2)
    rotate = coriolis[2:coriolis.shape[0] - 2]
    density = (-0.8 * temper + 0.6 * saline) * wet
    pressure = PRESS * jnp.cumsum(density, axis=0)
    press_x, press_y = gradients(pressure, wet)
    press_x = shrink(press_x, 1)
    press_y = shrink(press_y, 1)
    east_in = shrink(east_vel, 2)
    north_in = shrink(north_vel, 2)
    inner_mask = shrink(wet, 1)

    def mixing(field):
        slope_x, slope_y = gradients(field, wet)
        carried = east_in * shrink(slope_x, 1) + north_in * shrink(slope_y, 1)
        smoothed = laplacian(laplacian(field, wet), inner_mask)
        return -ADVECT * carried - KAPPA * smoothed

    east_tend = inner * (rotate * north_in - press_x + mixing(east_vel))
    north_tend = inner * (-rotate * east_in - press_y + mixing(north_vel))
    east_top = east_tend[:1] + WIND * inner[:1] * shrink(wind[0:1], 2)
    north_top = north_tend[:1] + WIND * inner[:1] * shrink(wind[1:2], 2)
    east_tend = jnp.concatenate([east_top, east_tend[1:]], axis=0)
    north_tend = jnp.concatenate([north_top, north_tend[1:]], axis=0)
    return east_tend, north_tend, inner * mixing(temper), inner * mixing(saline)


def corner_depth(depth, levels):
    smallest = jnp.minimum(jnp.minimum(depth[:-1, :-1], depth[:-1, 1:]), jnp.minimum(depth[1:, :-1], depth[1:, 1:]))
    return smallest.astype(jnp.float32) / levels


def diagonal_of(depth):
    return PHI + 0.5 * (depth[1:, 1:] + depth[1:, :-1] + depth[:-1, 1:] + depth[:-1, :-1])


def apply_operator(field, depth):
    low_left = field[:-1, :-1]
    low_right = field[:-1, 1:]
    up_left = field[1:, :-1]
    up_right = field[1:, 1:]
    slope_x = 0.5 * (low_right + up_right - low_left - up_left)
    slope_y = 0.5 * (up_left + up_right - low_left - low_right)
    flux_x = depth * slope_x
    flux_y = depth * slope_y
    spread = 0.5 * ((flux_x[1:, 1:] + flux_x[:-1, 1:]) - (flux_x[1:, :-1] + flux_x[:-1, :-1])
                    + (flux_y[1:, 1:] + flux_y[1:, :-1]) - (flux_y[:-1, 1:] + flux_y[:-1, :-1]))
    return PHI * field[1:-1, 1:-1] - spread


def pad_global(field, width):
    wrapped = jnp.concatenate([field[..., -width:], field, field[..., :width]], axis=-1)
    padding = [(0, 0)] * (field.ndim - 2) + [(width, width), (0, 0)]
    return jnp.pad(wrapped, padding)


def region(field, width):
    return field[4 - width:field.shape[0] - 4 + width, 4 - width:field.shape[1] - 4 + width]


def reference(eastward_flow, northward_flow, heat_anomaly, salt_anomaly, air_stress_forcing, earlier_sea_height_load, ocean_layer_depths):
    depth_pad = pad_global(ocean_layer_depths, 4)
    ocean_state_arrays = (eastward_flow, northward_flow, heat_anomaly, salt_anomaly)
    wet_two = wet_levels(region(depth_pad, 2), DEPTH_LAYERS)
    coriolis = coriolis_rows(-2, NORTHWARD_CELLS + 4, NORTHWARD_CELLS)
    wind_pad = pad_global(air_stress_forcing, 2)
    first = tendency(tuple(pad_global(item, 2) for item in ocean_state_arrays), wind_pad, wet_two, coriolis)
    provisional = tuple(item + extra for item, extra in zip(ocean_state_arrays, first))
    second = tendency(tuple(pad_global(item, 2) for item in provisional), wind_pad, wet_two, coriolis)
    updated = tuple(item + 0.5 * (term_first + term_second) for item, term_first, term_second in zip(ocean_state_arrays, first, second))
    wet_in = shrink(wet_two, 2)
    transport_east = jnp.sum(wet_in * updated[0], axis=0) / DEPTH_LAYERS
    transport_north = jnp.sum(wet_in * updated[1], axis=0) / DEPTH_LAYERS
    column_one = jnp.where(region(depth_pad, 1) > 0, 1.0, 0.0).astype(jnp.float32)
    slope_x = gradients(pad_global(transport_east, 1), column_one)[0]
    slope_y = gradients(pad_global(transport_north, 1), column_one)[1]
    forcing = shrink(column_one, 1) * (PHI * earlier_sea_height_load - DIVERGE * (slope_x + slope_y))
    depth_one = corner_depth(region(depth_pad, 1), DEPTH_LAYERS)
    diagonal = diagonal_of(depth_one)
    opening, updates = chebyshev_weights(ITERS)
    residual = forcing - apply_operator(pad_global(earlier_sea_height_load, 1), depth_one)
    direction = opening * (residual / diagonal)
    solution = earlier_sea_height_load
    for index in range(ITERS):
        solution = solution + direction
        if index + 1 < ITERS:
            residual = residual - apply_operator(pad_global(direction, 1), depth_one)
            keep, push = updates[index]
            direction = keep * direction + push * (residual / diagonal)
    return updated[0], updated[1], updated[2], updated[3], solution
```

```python
import functools
import math

import jax
import jax.numpy as jnp
from jax import lax
from jax.experimental import pallas as pl
from jax.experimental.pallas import tpu as pltpu
from jax.sharding import PartitionSpec as P

ITERS = 4
KAPPA = 0.004
ADVECT = 0.25
PRESS = 0.1
WIND = 0.5
PHI = 0.5
DIVERGE = 2.0
LOWER = 0.2
UPPER = 2.0

MESH = pl.DeviceIdType.MESH
FIELDS = 4
HALO = 4
SUB = 8
LANE = 128
AHEAD = 2
UNROLL = 2


def chebyshev_weights(count):
    middle = 0.5 * (UPPER + LOWER)
    half_span = 0.5 * (UPPER - LOWER)
    ratio_value = middle / half_span
    rho_now = 1.0 / ratio_value
    updates = []
    for _ in range(count - 1):
        rho_next = 1.0 / (2.0 * ratio_value - rho_now)
        updates.append((rho_next * rho_now, 2.0 * rho_next / half_span))
        rho_now = rho_next
    return 1.0 / middle, updates


def east(x):
    return pltpu.roll(x, x.shape[1] - 1, 1)


def west(x):
    return pltpu.roll(x, 1, 1)


def north(x):
    return pltpu.roll(x, x.shape[0] - 1, 0)


def south(x):
    return pltpu.roll(x, 1, 0)


def slot_lane(field, row):
    return (field % 2) * 64 + row * 8 + (field // 2) * 4


def turn(x, shift):
    shift = shift % LANE
    return x if shift == 0 else pltpu.roll(x, shift, 1)


def rows_loop(first, last, unroll, body):
    count = last - first
    assert count % unroll == 0

    def step(index, carry):
        for k in range(unroll):
            body(first + index * unroll + k)
        return carry

    lax.fori_loop(0, count // unroll, step, 0)


def kernel(
    levels, total_rows, by_count, bx_count,
    u_in, v_in, t_in, s_in, wind_in, ssh_in, depth_in,
    u_out, v_out, t_out, s_out, surface_out,
    own, ext, pack_send, pack_recv, corner_send, corner_recv, edge,
    lap, mix, press, mid, acc, carry_one, carry_two,
    depth_c, depth_e, depth_n, stress, cor,
    flow_sum, moved, moved_halo, flat,
    in_sem, out_sem, row_send, row_recv, pack_ss, pack_rs, corner_ss, corner_rs,
    moved_ss, moved_rs,
):
    inputs = (u_in, v_in, t_in, s_in)
    outputs = (u_out, v_out, t_out, s_out)
    rows = SUB
    span = rows + 2 * HALO
    width = ext.shape[-1]
    cols = width - LANE
    tiles = cols // LANE
    groups = -(-levels // SUB)
    flat_group = groups
    block = SUB * rows
    by = lax.axis_index("by")
    bx = lax.axis_index("bx")
    to_north = (lax.rem(by + 1, by_count), bx)
    to_south = (lax.rem(by + by_count - 1, by_count), bx)
    to_east = (by, lax.rem(bx + 1, bx_count))
    to_west = (by, lax.rem(bx + bx_count - 1, bx_count))

    def load_copy(field, tile):
        return pltpu.make_async_copy(
            inputs[field].at[:, pl.ds(tile * LANE, LANE)],
            own.at[field, tile, pl.ds(0, levels * rows)],
            in_sem.at[field, tile],
        )

    for field in range(FIELDS):
        for tile in range(tiles):
            load_copy(field, tile).start()

    barrier = pltpu.get_barrier_semaphore()
    for device in (to_north, to_south, to_east, to_west):
        pl.semaphore_signal(barrier, inc=1, device_id=device, device_id_type=MESH)

    base = groups * block
    for tile in range(tiles):
        lanes = slice(tile * LANE, (tile + 1) * LANE)
        own[0, tile, base : base + rows, :] = depth_in[:, lanes].astype(jnp.float32)
        own[0, tile, base + rows : base + 2 * rows, :] = ssh_in[:, lanes]
        own[0, tile, base + 2 * rows : base + 4 * rows, :] = wind_in[:, lanes]
        own[0, tile, base + 4 * rows : base + 8 * rows, :] = jnp.zeros((4 * rows, LANE), jnp.float32)
        if levels % SUB:
            pad = groups * block - levels * rows
            for field in range(FIELDS):
                own[field, tile, levels * rows : groups * block, :] = jnp.zeros((pad, LANE), jnp.float32)

    lane = lax.broadcasted_iota(jnp.int32, (SUB, LANE), 1)

    def stage(group, fields):
        west_pack = jnp.zeros((SUB, LANE), jnp.float32)
        east_pack = jnp.zeros((SUB, LANE), jnp.float32)
        for field in range(fields):
            for row in range(rows):
                parts = [
                    own[field, tile, pl.ds(group * block + row, SUB, stride=rows), :]
                    for tile in range(tiles)
                ]
                for tile in range(tiles):
                    ext[group, field, HALO + row, :, tile * LANE : (tile + 1) * LANE] = parts[tile]
                first = slot_lane(field, row)
                here = (lane >= first) & (lane < first + HALO)
                west_pack = jnp.where(here, turn(parts[0], first), west_pack)
                east_pack = jnp.where(here, turn(parts[-1], first + HALO), east_pack)
        pack_send[0, group] = west_pack
        pack_send[1, group] = east_pack

    def row_copy(group, fields, side):
        source = HALO + rows - HALO if side == 0 else HALO
        target = 0 if side == 0 else HALO + rows
        return pltpu.make_async_remote_copy(
            src_ref=ext.at[group, pl.ds(0, fields), pl.ds(source, HALO), :, pl.ds(0, cols)],
            dst_ref=ext.at[group, pl.ds(0, fields), pl.ds(target, HALO), :, pl.ds(0, cols)],
            send_sem=row_send.at[side, group],
            recv_sem=row_recv.at[side, group],
            device_id=to_north if side == 0 else to_south,
            device_id_type=MESH,
        )

    def pack_copy(side):
        return pltpu.make_async_remote_copy(
            src_ref=pack_send.at[side],
            dst_ref=pack_recv.at[1 - side],
            send_sem=pack_ss.at[side],
            recv_sem=pack_rs.at[1 - side],
            device_id=to_west if side == 0 else to_east,
            device_id_type=MESH,
        )

    def corner_copy(side):
        return pltpu.make_async_remote_copy(
            src_ref=corner_send.at[side],
            dst_ref=corner_recv.at[side],
            send_sem=corner_ss.at[side],
            recv_sem=corner_rs.at[side],
            device_id=to_north if side == 0 else to_south,
            device_id_type=MESH,
        )

    for field in range(FIELDS):
        for tile in range(tiles):
            load_copy(field, tile).wait()
    stage(flat_group, 1)
    pl.semaphore_wait(barrier, 4)
    for side in range(2):
        row_copy(flat_group, 1, side).start()
    for group in range(AHEAD):
        stage(group, FIELDS)
        for side in range(2):
            row_copy(group, FIELDS, side).start()

    def stage_step(group, carry):
        stage(group, FIELDS)
        return carry

    lax.fori_loop(AHEAD, groups, stage_step, 0)
    for side in range(2):
        pack_copy(side).start()

    row_index = by * rows - HALO + lax.broadcasted_iota(jnp.int32, (span, LANE), 0)
    turning = 1.2 * jnp.sin(0.9 * math.pi * ((row_index.astype(jnp.float32) + 0.5) / total_rows - 0.5))
    for row in range(span):
        one = jnp.broadcast_to(turning[row : row + 1, :], (SUB, LANE))
        for tile in range(width // LANE):
            cor[row, :, tile * LANE : (tile + 1) * LANE] = one

    for side in range(2):
        pack_copy(1 - side).wait_recv()
    own_lanes = (lane >= HALO * 8) & (lane < (HALO + rows) * 8)
    west_lanes = (lane & 7) < HALO

    def expand(group, fields):
        from_west = pack_recv[0, group]
        from_east = pack_recv[1, group]
        for_north = jnp.zeros((SUB, LANE), jnp.float32)
        for_south = jnp.zeros((SUB, LANE), jnp.float32)
        for field in range(fields):
            shift = HALO * 8 - slot_lane(field, 0)
            both = jnp.where(west_lanes, turn(from_west, shift), turn(from_east, shift + HALO))
            edge[group, field] = both
            part = (lane >= field * 32) & (lane < field * 32 + 32)
            for_north = jnp.where(part, turn(both, field * 32 - rows * 8), for_north)
            for_south = jnp.where(part, turn(both, field * 32 - HALO * 8), for_south)
        corner_send[0, group] = for_north
        corner_send[1, group] = for_south

    def expand_step(group, carry):
        expand(group, FIELDS)
        return carry

    expand(flat_group, 1)
    lax.fori_loop(0, groups, expand_step, 0)
    for side in range(2):
        corner_copy(side).start()

    def send_step(group, carry):
        for side in range(2):
            row_copy(group, FIELDS, side).start()
        return carry

    lax.fori_loop(AHEAD, groups, send_step, 0)

    for side in range(2):
        corner_copy(side).wait_recv()

    def widen(group, fields):
        from_south = corner_recv[0, group]
        from_north = corner_recv[1, group]
        for field in range(fields):
            all_rows = jnp.where(
                own_lanes,
                edge[group, field],
                jnp.where(lane < HALO * 8, turn(from_south, -32 * field), turn(from_north, 96 - 32 * field)),
            )
            for row in range(span):
                ext[group, field, row, :, cols:width] = turn(all_rows, LANE - HALO - 8 * row)

    for side in range(2):
        row_copy(flat_group, 1, side).wait_recv()
    widen(flat_group, 1)

    sub = lax.broadcasted_iota(jnp.int32, (SUB, width), 0)
    for row in range(span):
        index = by * rows + (row - HALO)
        inside = (index >= 0) & (index < total_rows)
        values = ext[flat_group, 0, row]
        here = jnp.where(inside, jnp.broadcast_to(values[0:1, :], (SUB, width)), 0.0)
        depth_c[row] = here
        depth_e[row] = jnp.minimum(here, east(here))
        for axis in range(2):
            stress[axis, row] = jnp.where(
                sub == 0, WIND * jnp.broadcast_to(values[2 + axis : 3 + axis, :], (SUB, width)), 0.0
            )
        carry_one[row] = jnp.zeros((SUB, width), jnp.float32)
        carry_two[row] = jnp.zeros((SUB, width), jnp.float32)
        place = (row + span - HALO) % span
        flat[0, place : place + 1, :] = here[0:1, :]
        flat[1, place : place + 1, :] = values[1:2, :]
    for row in range(span - 1):
        depth_n[row] = jnp.minimum(depth_c[row], depth_c[row + 1])
    for axis in range(2):
        for row in range(rows):
            flow_sum[axis, row] = jnp.zeros((SUB, cols), jnp.float32)

    depth = flat[0]
    ssh = flat[1]
    near = jnp.minimum(depth, east(depth))
    corner = jnp.minimum(near, north(near)) * (1.0 / levels)
    pair = corner + west(corner)
    diagonal_inverse = 1.0 / (PHI + 0.5 * (pair + south(pair)))
    ocean = jnp.where(depth > 0.0, 1.0, 0.0)

    def operator(field, corner):
        total = field + north(field)
        change = north(field) - field
        flux_x = corner * (0.5 * (east(total) - total))
        flux_y = corner * (0.5 * (east(change) + change))
        along_x = flux_x + south(flux_x)
        along_y = flux_y + west(flux_y)
        return PHI * field - 0.5 * ((along_x - west(along_x)) + (along_y - south(along_y)))

    flat[2] = corner
    flat[3] = diagonal_inverse
    flat[4] = ocean
    flat[5] = ocean * (PHI * ssh) - operator(ssh, corner)

    level = lax.broadcasted_iota(jnp.int32, (SUB, width), 0).astype(jnp.float32)

    def masks(group, row):
        number = level + (group * SUB).astype(jnp.float32)
        return (
            number < depth_c[row], number < depth_e[row],
            number < depth_n[row], number < depth_n[row - 1],
        )

    def first_half(state, row, group, carry):
        wet, wet_e, wet_n, wet_s = masks(group, row)
        east_vel = state(0, row)
        north_vel = state(1, row)
        for field in range(FIELDS):
            here = state(field, row)
            face_e = jnp.where(wet_e, east(here) - here, 0.0)
            face_w = west(face_e)
            face_n = jnp.where(wet_n, state(field, row + 1) - here, 0.0)
            face_s = jnp.where(wet_s, here - state(field, row - 1), 0.0)
            lap[field, row] = (face_e - face_w) + (face_n - face_s)
            mix[field, row] = (-0.5 * ADVECT) * (east_vel * (face_e + face_w) + north_vel * (face_n + face_s))
        density = jnp.where(wet, (-0.8 * PRESS) * state(2, row) + (0.6 * PRESS) * state(3, row), 0.0)
        running = density
        total = density
        for shift in (1, 2, 4):
            running = running + jnp.where(sub >= shift, pltpu.roll(running, shift, 0), 0.0)
            total = total + pltpu.roll(total, shift, 0)
        press[row] = carry[row] + running
        carry[row] = carry[row] + total

    def second_half(state, row, group, keep):
        wet, wet_e, wet_n, wet_s = masks(group, row)

        def faces(ref_row):
            here = ref_row(row)
            face_e = jnp.where(wet_e, east(here) - here, 0.0)
            face_n = jnp.where(wet_n, ref_row(row + 1) - here, 0.0)
            face_s = jnp.where(wet_s, here - ref_row(row - 1), 0.0)
            return face_e[:, :keep], west(face_e)[:, :keep], face_n[:, :keep], face_s[:, :keep]

        press_e, press_w, press_n, press_s = faces(lambda r: press[r])
        turned = cor[row][:, :keep]
        top = (group == 0).astype(jnp.float32)
        forced = (
            turned * state(1, row)[:, :keep] + top * stress[0, row][:, :keep],
            -turned * state(0, row)[:, :keep] + top * stress[1, row][:, :keep],
        )
        forced = [jnp.where(wet[:, :keep], item, 0.0) for item in forced]
        forced[0] = forced[0] - 0.5 * (press_e + press_w)
        forced[1] = forced[1] - 0.5 * (press_n + press_s)
        result = []
        for field in range(FIELDS):
            face_e, face_w, face_n, face_s = faces(lambda r: lap[field, r])
            change = mix[field, row][:, :keep] - KAPPA * ((face_e - face_w) + (face_n - face_s))
            result.append(change + forced[field] if field < 2 else change)
        return result

    def out_copy(group, field, tile, count):
        return pltpu.make_async_copy(
            own.at[field, tile, pl.ds(pl.multiple_of(group * block, block), count)],
            outputs[field].at[pl.ds(pl.multiple_of(group * block, block), count), pl.ds(tile * LANE, LANE)],
            out_sem.at[field, tile],
        )

    last_count = levels * rows - (groups - 1) * block

    def group_step(group, carry):
        for side in range(2):
            row_copy(group, FIELDS, side).wait_recv()
        widen(group, FIELDS)

        def given(field, row):
            return ext[group, field, row]

        def provisional(field, row):
            return mid[field, row]

        def pass_one(row):
            first_half(given, row, group, carry_one)

        def pass_two(row):
            first = second_half(given, row, group, width)
            for field in range(FIELDS):
                mid[field, row] = ext[group, field, row] + first[field]

        def pass_three(row):
            first_half(provisional, row, group, carry_two)

        def pass_four(row):
            second = second_half(provisional, row, group, cols)
            inner = row - HALO
            wet = (level + (group * SUB).astype(jnp.float32))[:, :cols] < depth_c[row][:, :cols]
            for field in range(FIELDS):
                value = 0.5 * (ext[group, field, row][:, :cols] + mid[field, row][:, :cols] + second[field])
                for tile in range(tiles):
                    own[field, tile, pl.ds(group * block + inner, SUB, stride=rows), :] = value[
                        :, tile * LANE : (tile + 1) * LANE
                    ]
                if field < 2:
                    flow_sum[field, inner] = flow_sum[field, inner] + jnp.where(wet, value, 0.0)

        rows_loop(1, span - 1, UNROLL, pass_one)
        rows_loop(2, span - 2, UNROLL, pass_two)
        rows_loop(3, span - 3, UNROLL, pass_three)
        rows_loop(HALO, HALO + rows, UNROLL, pass_four)

        @pl.when(group < groups - 1)
        def _():
            for field in range(FIELDS):
                for tile in range(tiles):
                    out_copy(group, field, tile, block).start()

        @pl.when(group == groups - 1)
        def _():
            for field in range(FIELDS):
                for tile in range(tiles):
                    out_copy(group, field, tile, last_count).start()

        return carry

    lax.fori_loop(0, groups, group_step, 0)

    for axis in range(2):
        for row in range(rows):
            moved[axis, row : row + 1, :cols] = jnp.sum(flow_sum[axis, row], axis=0, keepdims=True) * (1.0 / levels)

    def moved_column_copy(side):
        tile = 0 if side == 0 else tiles - 1
        return pltpu.make_async_remote_copy(
            src_ref=moved.at[:, :, pl.ds(tile * LANE, LANE)],
            dst_ref=moved_halo.at[1 - side, :, :, pl.ds(0, LANE)],
            send_sem=moved_ss.at[side],
            recv_sem=moved_rs.at[1 - side],
            device_id=to_west if side == 0 else to_east,
            device_id_type=MESH,
        )

    def moved_row_copy(side):
        return pltpu.make_async_remote_copy(
            src_ref=moved,
            dst_ref=moved_halo.at[2 + side],
            send_sem=moved_ss.at[2 + side],
            recv_sem=moved_rs.at[2 + side],
            device_id=to_north if side == 0 else to_south,
            device_id_type=MESH,
        )

    for side in range(2):
        moved_column_copy(side).start()
    for side in range(2):
        moved_column_copy(1 - side).wait_recv()
    for axis in range(2):
        moved[axis, :, cols:width] = jnp.where(
            lane < LANE // 2, moved_halo[1, axis, :, :LANE], moved_halo[0, axis, :, :LANE]
        )
    for side in range(2):
        moved_row_copy(side).start()
    for side in range(2):
        moved_row_copy(side).wait_recv()
    lower = lax.broadcasted_iota(jnp.int32, (SUB, width), 0) < HALO
    transports = [
        jnp.concatenate([moved[axis], jnp.where(lower, moved_halo[3, axis], moved_halo[2, axis])], axis=0)
        for axis in range(2)
    ]

    corner = flat[2]
    diagonal_inverse = flat[3]
    ocean = flat[4]
    face_x = ocean * east(ocean) * (east(transports[0]) - transports[0])
    face_y = ocean * north(ocean) * (north(transports[1]) - transports[1])
    spread = 0.5 * ((face_x + west(face_x)) + (face_y + south(face_y)))
    residual = flat[5] - (DIVERGE * ocean) * spread
    opening, updates = chebyshev_weights(ITERS)
    direction = opening * (residual * diagonal_inverse)
    surface = flat[1]
    for index in range(ITERS):
        surface = surface + direction
        if index + 1 < ITERS:
            residual = residual - operator(direction, corner)
            keep, push = updates[index]
            direction = keep * direction + push * (residual * diagonal_inverse)
    surface_out[...] = surface[:rows, :cols]

    for field in range(FIELDS):
        for tile in range(tiles):
            for group in range(groups):
                out_copy(group, field, tile, block if group < groups - 1 else last_count).wait()
    for side in range(2):
        pack_copy(side).wait_send()
        corner_copy(side).wait_send()
        moved_column_copy(side).wait_send()
        moved_row_copy(side).wait_send()
        row_copy(flat_group, 1, side).wait_send()

    def drain(group, carry):
        for side in range(2):
            row_copy(group, FIELDS, side).wait_send()
        return carry

    lax.fori_loop(0, groups, drain, 0)


def body(by_count, bx_count, u, v, t, s, wind, ssh, depth):
    levels, rows, cols = u.shape
    groups = -(-levels // SUB)
    span = rows + 2 * HALO
    width = cols + LANE
    f32 = jnp.float32
    flat_shape = (levels * rows, cols)
    args = [item.reshape(flat_shape) for item in (u, v, t, s)]
    outs = pl.pallas_call(
        functools.partial(kernel, levels, rows * by_count, by_count, bx_count),
        out_shape=[jax.ShapeDtypeStruct(flat_shape, f32)] * FIELDS + [jax.ShapeDtypeStruct(ssh.shape, f32)],
        in_specs=[pl.BlockSpec(memory_space=pl.ANY)] * FIELDS + [pl.BlockSpec(memory_space=pltpu.VMEM)] * 3,
        out_specs=[pl.BlockSpec(memory_space=pl.ANY)] * FIELDS + [pl.BlockSpec(memory_space=pltpu.VMEM)],
        scratch_shapes=[
            pltpu.VMEM((FIELDS, cols // LANE, (groups + 1) * SUB * rows, LANE), f32),
            pltpu.VMEM((groups + 1, FIELDS, span, SUB, width), f32),
            pltpu.VMEM((2, groups + 1, SUB, LANE), f32),
            pltpu.VMEM((2, groups + 1, SUB, LANE), f32),
            pltpu.VMEM((2, groups + 1, SUB, LANE), f32),
            pltpu.VMEM((2, groups + 1, SUB, LANE), f32),
            pltpu.VMEM((groups + 1, FIELDS, SUB, LANE), f32),
            pltpu.VMEM((FIELDS, span, SUB, width), f32),
            pltpu.VMEM((FIELDS, span, SUB, width), f32),
            pltpu.VMEM((span, SUB, width), f32),
            pltpu.VMEM((FIELDS, span, SUB, width), f32),
            pltpu.VMEM((SUB, LANE), f32),
            pltpu.VMEM((span, SUB, width), f32),
            pltpu.VMEM((span, SUB, width), f32),
            pltpu.VMEM((span, SUB, width), f32),
            pltpu.VMEM((span, SUB, width), f32),
            pltpu.VMEM((span, SUB, width), f32),
            pltpu.VMEM((2, span, SUB, width), f32),
            pltpu.VMEM((span, SUB, width), f32),
            pltpu.VMEM((2, rows, SUB, cols), f32),
            pltpu.VMEM((2, rows, width), f32),
            pltpu.VMEM((4, 2, rows, width), f32),
            pltpu.VMEM((6, span, width), f32),
            pltpu.SemaphoreType.DMA((FIELDS, cols // LANE)),
            pltpu.SemaphoreType.DMA((FIELDS, cols // LANE)),
            pltpu.SemaphoreType.DMA((2, groups + 1)),
            pltpu.SemaphoreType.DMA((2, groups + 1)),
            pltpu.SemaphoreType.DMA((2,)),
            pltpu.SemaphoreType.DMA((2,)),
            pltpu.SemaphoreType.DMA((2,)),
            pltpu.SemaphoreType.DMA((2,)),
            pltpu.SemaphoreType.DMA((4,)),
            pltpu.SemaphoreType.DMA((4,)),
        ],
        compiler_params=pltpu.CompilerParams(
            collective_id=0, has_side_effects=True, vmem_limit_bytes=40 << 20
        ),
    )(*args, wind.reshape(2 * rows, cols), ssh, depth)
    return tuple(item.reshape(u.shape) for item in outs[:FIELDS]) + (outs[FIELDS],)


def solution(mesh):
    whole = P(None, "by", "bx")
    flat = P("by", "bx")
    return jax.shard_map(
        functools.partial(body, mesh.shape["by"], mesh.shape["bx"]),
        mesh=mesh,
        in_specs=(whole,) * 5 + (flat, flat),
        out_specs=(whole,) * 4 + (flat,),
        check_vma=False,
    )
```

```python
import functools
import math

import jax
import jax.numpy as jnp
from jax import lax
from jax.experimental import pallas as pl
from jax.experimental.pallas import tpu as pltpu
from jax.sharding import PartitionSpec as P

ITERS = 4
KAPPA = 0.004
ADVECT = 0.25
PRESS = 0.1
WIND = 0.5
PHI = 0.5
DIVERGE = 2.0
LOWER = 0.2
UPPER = 2.0

MESH = pl.DeviceIdType.MESH
FIELDS = 4
HALO = 4
SUB = 8
LANE = 128
AHEAD = 3
FIRST = 5
SECOND = 4
FINISH = 4


def chebyshev_weights(count):
    middle = 0.5 * (UPPER + LOWER)
    half_span = 0.5 * (UPPER - LOWER)
    ratio_value = middle / half_span
    rho_now = 1.0 / ratio_value
    updates = []
    for _ in range(count - 1):
        rho_next = 1.0 / (2.0 * ratio_value - rho_now)
        updates.append((rho_next * rho_now, 2.0 * rho_next / half_span))
        rho_now = rho_next
    return 1.0 / middle, updates


def east(x):
    return pltpu.roll(x, x.shape[1] - 1, 1)


def west(x):
    return pltpu.roll(x, 1, 1)


def north(x):
    return pltpu.roll(x, x.shape[0] - 1, 0)


def south(x):
    return pltpu.roll(x, 1, 0)


def slot_lane(field, row):
    return (field % 2) * 64 + row * 8 + (field // 2) * 4


def turn(x, shift):
    shift = shift % LANE
    return x if shift == 0 else pltpu.roll(x, shift, 1)


def kernel(
    levels, total_rows, by_count, bx_count,
    u_in, v_in, t_in, s_in, wind_in, ssh_in, depth_in,
    own, surface_out,
    ext, depth_own, pack_send, pack_recv, corner_send, corner_recv, edge,
    lap, mix, press, depth_c, depth_e, depth_n, stress, cor,
    flow_sum, moved, moved_rows, moved_cols, moved_corners, flat,
    in_sem, row_send, row_recv, pack_ss, pack_rs, corner_ss, corner_rs, moved_ss, moved_rs,
):
    inputs = (u_in, v_in, t_in, s_in)
    rows = SUB
    span = rows + 2 * HALO
    width = ext.shape[-1]
    cols = width - LANE
    tiles = cols // LANE
    groups = -(-levels // SUB)
    block = SUB * rows
    base = groups * block
    by = lax.axis_index("by")
    bx = lax.axis_index("bx")

    def device(step_y, step_x):
        return (lax.rem(by + step_y + by_count, by_count), lax.rem(bx + step_x + bx_count, bx_count))

    neighbours = [(y, x) for y in (-1, 0, 1) for x in (-1, 0, 1) if (y, x) != (0, 0)]

    def load_copies():
        result = []
        for tile in range(tiles):
            lanes = pl.ds(tile * LANE, LANE)
            for field in range(FIELDS):
                result.append(pltpu.make_async_copy(
                    inputs[field].at[:, lanes], own.at[field, tile, pl.ds(0, levels * rows)], in_sem.at[tile, field]
                ))
            result.append(pltpu.make_async_copy(
                ssh_in.at[:, lanes], own.at[0, tile, pl.ds(base + rows, rows)], in_sem.at[tile, FIELDS]
            ))
            result.append(pltpu.make_async_copy(
                wind_in.at[:, lanes], own.at[0, tile, pl.ds(base + 2 * rows, 2 * rows)], in_sem.at[tile, FIELDS + 1]
            ))
        result.append(pltpu.make_async_copy(depth_in, depth_own, in_sem.at[0, FIELDS + 2]))
        return result

    for copy in load_copies():
        copy.start()

    barrier = pltpu.get_barrier_semaphore()
    for step in neighbours:
        pl.semaphore_signal(barrier, inc=1, device_id=device(*step), device_id_type=MESH)

    lane = lax.broadcasted_iota(jnp.int32, (SUB, LANE), 1)
    for tile in range(tiles):
        for field in range(FIELDS):
            if levels % SUB:
                pad = base - levels * rows
                own[field, tile, levels * rows : base, :] = jnp.zeros((pad, LANE), jnp.float32)
        own[0, tile, base + 4 * rows : base + block, :] = jnp.zeros((block - 4 * rows, LANE), jnp.float32)

    def row_copy(group, fields, side):
        source = HALO + rows - HALO if side == 0 else HALO
        target = 0 if side == 0 else HALO + rows
        return pltpu.make_async_remote_copy(
            src_ref=ext.at[group, pl.ds(0, fields), pl.ds(source, HALO), :, pl.ds(0, cols)],
            dst_ref=ext.at[group, pl.ds(0, fields), pl.ds(target, HALO), :, pl.ds(0, cols)],
            send_sem=row_send.at[side, group],
            recv_sem=row_recv.at[side, group],
            device_id=device(1 - 2 * side, 0),
            device_id_type=MESH,
        )

    def pack_copy(side):
        return pltpu.make_async_remote_copy(
            src_ref=pack_send.at[side],
            dst_ref=pack_recv.at[1 - side],
            send_sem=pack_ss.at[side],
            recv_sem=pack_rs.at[1 - side],
            device_id=device(0, 2 * side - 1),
            device_id_type=MESH,
        )

    def corner_copy(side):
        return pltpu.make_async_remote_copy(
            src_ref=corner_send.at[side],
            dst_ref=corner_recv.at[side],
            send_sem=corner_ss.at[side],
            recv_sem=corner_rs.at[side],
            device_id=device(1 - 2 * side, 0),
            device_id_type=MESH,
        )

    def group_of(index):
        return lax.rem(index + groups, groups + 1)

    for copy in load_copies():
        copy.wait()
    for tile in range(tiles):
        own[0, tile, base : base + rows, :] = depth_own[:, tile * LANE : (tile + 1) * LANE].astype(jnp.float32)
    pl.semaphore_wait(barrier, len(neighbours))

    def stage_step(index, carry):
        group = group_of(index)
        west_pack = jnp.zeros((SUB, LANE), jnp.float32)
        east_pack = jnp.zeros((SUB, LANE), jnp.float32)
        for field in range(FIELDS):
            for row in range(rows):
                parts = [
                    own[field, tile, pl.ds(group * block + row, SUB, stride=rows), :]
                    for tile in range(tiles)
                ]
                for tile in range(tiles):
                    ext[group, field, HALO + row, :, tile * LANE : (tile + 1) * LANE] = parts[tile]
                first = slot_lane(field, row)
                here = (lane >= first) & (lane < first + HALO)
                west_pack = jnp.where(here, turn(parts[0], first), west_pack)
                east_pack = jnp.where(here, turn(parts[-1], first + HALO), east_pack)
        pack_send[0, group] = west_pack
        pack_send[1, group] = east_pack

        @pl.when(index == 0)
        def _():
            for side in range(2):
                row_copy(groups, 1, side).start()

        @pl.when(index == 1)
        def _():
            for side in range(2):
                row_copy(group, FIELDS, side).start()

        return carry

    lax.fori_loop(0, groups + 1, stage_step, 0)
    for side in range(2):
        pack_copy(side).start()

    row_index = by * rows - HALO + lax.broadcasted_iota(jnp.int32, (span, LANE), 0)
    turning = 1.2 * jnp.sin(0.9 * math.pi * ((row_index.astype(jnp.float32) + 0.5) / total_rows - 0.5))
    for row in range(span):
        cor[row] = jnp.broadcast_to(turning[row : row + 1, :], (SUB, LANE))

    for side in range(2):
        pack_copy(1 - side).wait_recv()
    own_lanes = (lane >= HALO * 8) & (lane < (HALO + rows) * 8)
    west_lanes = (lane & 7) < HALO

    def expand_step(group, carry):
        from_west = pack_recv[0, group]
        from_east = pack_recv[1, group]
        for_north = jnp.zeros((SUB, LANE), jnp.float32)
        for_south = jnp.zeros((SUB, LANE), jnp.float32)
        for field in range(FIELDS):
            shift = HALO * 8 - slot_lane(field, 0)
            both = jnp.where(west_lanes, turn(from_west, shift), turn(from_east, shift + HALO))
            edge[group, field] = both
            part = (lane >= field * 32) & (lane < field * 32 + 32)
            for_north = jnp.where(part, turn(both, field * 32 - rows * 8), for_north)
            for_south = jnp.where(part, turn(both, field * 32 - HALO * 8), for_south)
        corner_send[0, group] = for_north
        corner_send[1, group] = for_south
        return carry

    lax.fori_loop(0, groups + 1, expand_step, 0)
    for side in range(2):
        corner_copy(side).start()

    def send_step(group, carry):
        for side in range(2):
            row_copy(group, FIELDS, side).start()
        return carry

    lax.fori_loop(1, AHEAD, send_step, 0)

    sub = lax.broadcasted_iota(jnp.int32, (SUB, width), 0)
    level = sub.astype(jnp.float32)
    zeros = jnp.zeros((SUB, width), jnp.float32)

    def clear_step(row, carry):
        press[0, row] = zeros
        press[1, row] = zeros
        return carry

    lax.fori_loop(0, span, clear_step, 0)
    for axis in range(2):
        for row in range(rows):
            flow_sum[axis, row] = jnp.zeros((SUB, cols), jnp.float32)

    for side in range(2):
        corner_copy(side).wait_recv()

    def operator(field, corner):
        north_field = north(field)
        total = field + north_field
        change = north_field - field
        flux_x = corner * (0.5 * (east(total) - total))
        flux_y = corner * (0.5 * (east(change) + change))
        along_x = flux_x + south(flux_x)
        along_y = flux_y + west(flux_y)
        return PHI * field - 0.5 * ((along_x - west(along_x)) + (along_y - south(along_y)))

    def flat_tables():
        def table_step(row, carry):
            index = by * rows + (row - HALO)
            inside = (index >= 0) & (index < total_rows)
            here = jnp.where(inside, jnp.broadcast_to(ext[groups, 0, row, 0:1, :], (SUB, width)), 0.0)
            depth_c[row] = here
            depth_e[row] = jnp.minimum(here, east(here))
            for axis in range(2):
                wind = jnp.broadcast_to(ext[groups, 0, row, 2 + axis : 3 + axis, :], (SUB, width))
                stress[axis, row] = jnp.where(sub == 0, WIND * wind, 0.0)
            place = lax.rem(row + span - HALO, span)
            flat[0, pl.ds(place, 1), :] = here[0:1, :]
            flat[1, pl.ds(place, 1), :] = ext[groups, 0, row, 1:2, :]
            return carry

        lax.fori_loop(0, span, table_step, 0)

        def face_step(row, carry):
            depth_n[row] = jnp.minimum(depth_c[row], depth_c[row + 1])
            return carry

        lax.fori_loop(0, span - 1, face_step, 0)
        depth = flat[0]
        ssh = flat[1]
        near = jnp.minimum(depth, east(depth))
        corner = jnp.minimum(near, north(near)) * (1.0 / levels)
        pair = corner + west(corner)
        ocean = jnp.where(depth > 0.0, 1.0, 0.0)
        flat[2] = corner
        flat[3] = 1.0 / (PHI + 0.5 * (pair + south(pair)))
        flat[4] = ocean
        flat[5] = ocean * (PHI * ssh) - operator(ssh, corner)

    def cut(mask, value):
        return jnp.where(mask, value, 0.0)

    def tendencies(group):
        number = level + (group * SUB).astype(jnp.float32)

        def stage_pass(part, carry):
            slot = jnp.where(part == 0, group, groups + part)
            after = groups + 1 + part

            def first_block(index, inner):
                row = 1 + 2 * part + index * FIRST
                wet = [number < depth_c[row + k] for k in range(FIRST)]
                wet_e = [number < depth_e[row + k] for k in range(FIRST)]
                wet_n = [number < depth_n[row - 1 + k] for k in range(FIRST + 1)]
                speed = [
                    [(-0.5 * ADVECT) * ext[slot, field, row + k] for field in range(2)] for k in range(FIRST)
                ]
                for field in range(FIELDS):
                    cells = [ext[slot, field, row - 1 + k] for k in range(FIRST + 2)]
                    faces = [cut(wet_n[k], cells[k + 1] - cells[k]) for k in range(FIRST + 1)]
                    for k in range(FIRST):
                        here = cells[k + 1]
                        face_e = cut(wet_e[k], east(here) - here)
                        face_w = west(face_e)
                        lap[field, row + k] = (face_e - face_w) + (faces[k + 1] - faces[k])
                        mix[field, row + k] = speed[k][0] * (face_e + face_w) + speed[k][1] * (
                            faces[k + 1] + faces[k]
                        )
                above = [
                    jnp.broadcast_to(press[part, row + k, SUB - 1 : SUB, :], (SUB, width)) for k in range(FIRST)
                ]
                for k in range(FIRST):
                    running = cut(
                        wet[k],
                        (-0.8 * PRESS) * ext[slot, 2, row + k] + (0.6 * PRESS) * ext[slot, 3, row + k],
                    )
                    for shift in (1, 2, 4):
                        running = running + jnp.where(sub >= shift, pltpu.roll(running, shift, 0), 0.0)
                    press[part, row + k] = above[k] + running
                return inner

            def second_block(index, inner):
                row = 2 + 2 * part + index * SECOND
                wet = [number < depth_c[row + k] for k in range(SECOND)]
                wet_e = [number < depth_e[row + k] for k in range(SECOND)]
                wet_n = [number < depth_n[row - 1 + k] for k in range(SECOND + 1)]
                cells = [press[part, row - 1 + k] for k in range(SECOND + 2)]
                faces = [cut(wet_n[k], cells[k + 1] - cells[k]) for k in range(SECOND + 1)]
                forced = []
                for k in range(SECOND):
                    here = cells[k + 1]
                    face_e = cut(wet_e[k], east(here) - here)
                    turned = jnp.concatenate([cor[row + k]] * (width // LANE), axis=1)
                    forced.append((
                        cut(wet[k], turned * ext[slot, 1, row + k]) - 0.5 * (face_e + west(face_e)),
                        cut(wet[k], -turned * ext[slot, 0, row + k]) - 0.5 * (faces[k + 1] + faces[k]),
                    ))
                results = []
                for field in range(FIELDS):
                    cells = [lap[field, row - 1 + k] for k in range(SECOND + 2)]
                    faces = [cut(wet_n[k], cells[k + 1] - cells[k]) for k in range(SECOND + 1)]
                    for k in range(SECOND):
                        here = cells[k + 1]
                        face_e = cut(wet_e[k], east(here) - here)
                        twice = (face_e - west(face_e)) + (faces[k + 1] - faces[k])
                        value = (ext[slot, field, row + k] + mix[field, row + k]) - KAPPA * twice
                        results.append((field, row + k, value + forced[k][field] if field < 2 else value))
                for field, place, value in results:
                    ext[after, field, place] = value
                return inner

            lax.fori_loop(0, (span - 2 - 4 * part + FIRST - 1) // FIRST, first_block, 0)
            lax.fori_loop(0, (span - 4 - 4 * part + SECOND - 1) // SECOND, second_block, 0)
            def wind_step(row, inner):
                for axis in range(2):
                    ext[after, axis, row] = ext[after, axis, row] + cut(number < depth_c[row], stress[axis, row])
                return inner

            @pl.when(group == 0)
            def _():
                lax.fori_loop(2 + 2 * part, span - 2 - 2 * part, wind_step, 0)

            return carry

        lax.fori_loop(0, 2, stage_pass, 0)

        def finish_block(index, carry):
            for k in range(FINISH):
                row = index * FINISH + k
                wet = (number < depth_c[row + HALO])[:, :cols]
                for field in range(FIELDS):
                    value = 0.5 * (
                        ext[group, field, row + HALO, :, :cols] + ext[groups + 2, field, row + HALO, :, :cols]
                    )
                    for tile in range(tiles):
                        own[field, tile, pl.ds(group * block + row, SUB, stride=rows), :] = value[
                            :, tile * LANE : (tile + 1) * LANE
                        ]
                    if field < 2:
                        flow_sum[field, row] = flow_sum[field, row] + cut(wet, value)
            return carry

        lax.fori_loop(0, rows // FINISH, finish_block, 0)

    def group_step(index, carry):
        group = group_of(index)

        @pl.when(index == 0)
        def _():
            for side in range(2):
                row_copy(groups, 1, side).wait_recv()

        @pl.when(index > 0)
        def _():
            for side in range(2):
                row_copy(group, FIELDS, side).wait_recv()

        @pl.when((index > 0) & (index <= groups - AHEAD))
        def _():
            for side in range(2):
                row_copy(group + AHEAD, FIELDS, side).start()

        from_south = corner_recv[0, group]
        from_north = corner_recv[1, group]
        for field in range(FIELDS):
            all_rows = jnp.where(
                own_lanes,
                edge[group, field],
                jnp.where(lane < HALO * 8, turn(from_south, -32 * field), turn(from_north, 96 - 32 * field)),
            )
            for row in range(span):
                ext[group, field, row, :, cols:width] = turn(all_rows, LANE - HALO - 8 * row)

        @pl.when(index == 0)
        def _():
            flat_tables()

        @pl.when(index > 0)
        def _():
            tendencies(group)

        return carry

    lax.fori_loop(0, groups + 1, group_step, 0)

    def total_step(row, carry):
        for axis in range(2):
            total = jnp.sum(flow_sum[axis, row], axis=0, keepdims=True) * (1.0 / levels)
            moved[axis, pl.ds(row, 1), :] = total
        return carry

    lax.fori_loop(0, rows, total_step, 0)

    def moved_copy(step):
        y, x = step
        place = neighbours.index(step)
        other = neighbours.index((-y, -x))
        if x == 0:
            source, target = moved, moved_rows.at[(1 - y) // 2]
        else:
            tile = tiles - 1 if x > 0 else 0
            source = moved.at[:, :, pl.ds(tile * LANE, LANE)]
            side = (1 - x) // 2
            target = moved_cols.at[side] if y == 0 else moved_corners.at[(1 - y) // 2, side]
        return pltpu.make_async_remote_copy(
            src_ref=source, dst_ref=target, send_sem=moved_ss.at[place], recv_sem=moved_rs.at[place],
            device_id=device(y, x), device_id_type=MESH,
        )

    for step in neighbours:
        moved_copy(step).start()
    for step in neighbours:
        moved_copy(step).wait_recv()
    lower = lax.broadcasted_iota(jnp.int32, (SUB, cols), 0) < HALO
    lower_tile = lax.broadcasted_iota(jnp.int32, (SUB, LANE), 0) < HALO
    right = lane < LANE // 2
    transports = []
    for axis in range(2):
        near = jnp.concatenate(
            [moved[axis], jnp.where(right, moved_cols[1, axis], moved_cols[0, axis])], axis=1
        )
        corners = [
            jnp.where(right, moved_corners[side, 1, axis], moved_corners[side, 0, axis]) for side in range(2)
        ]
        far = jnp.concatenate(
            [
                jnp.where(lower, moved_rows[1, axis], moved_rows[0, axis]),
                jnp.where(lower_tile, corners[1], corners[0]),
            ],
            axis=1,
        )
        transports.append(jnp.concatenate([near, far], axis=0))

    corner = flat[2]
    diagonal_inverse = flat[3]
    ocean = flat[4]
    face_x = ocean * east(ocean) * (east(transports[0]) - transports[0])
    face_y = ocean * north(ocean) * (north(transports[1]) - transports[1])
    spread = 0.5 * ((face_x + west(face_x)) + (face_y + south(face_y)))
    residual = flat[5] - (DIVERGE * ocean) * spread
    opening, updates = chebyshev_weights(ITERS)
    direction = opening * (residual * diagonal_inverse)

    def pick(index, values):
        result = jnp.float32(values[-1])
        for k in range(len(values) - 1):
            result = jnp.where(index == k, jnp.float32(values[k]), result)
        return result

    def solve_step(index, carry):
        surface, residual, direction = carry
        surface = surface + direction
        residual = residual - operator(direction, corner)
        keep = pick(index, [item[0] for item in updates])
        push = pick(index, [item[1] for item in updates])
        direction = keep * direction + push * (residual * diagonal_inverse)
        return surface, residual, direction

    surface, residual, direction = lax.fori_loop(0, ITERS - 1, solve_step, (flat[1], residual, direction))
    surface_out[...] = (surface + direction)[:rows, :cols]

    for side in range(2):
        pack_copy(side).wait_send()
        corner_copy(side).wait_send()
        row_copy(groups, 1, side).wait_send()
    for step in neighbours:
        moved_copy(step).wait_send()

    def drain(group, carry):
        for side in range(2):
            row_copy(group, FIELDS, side).wait_send()
        return carry

    lax.fori_loop(0, groups, drain, 0)


def deliver(levels, fields_in, surface_in, u_out, v_out, t_out, s_out, surface_out, sems):
    outputs = (u_out, v_out, t_out, s_out)
    count = u_out.shape[0]
    copies = [
        pltpu.make_async_copy(
            fields_in.at[field, tile, pl.ds(0, count)],
            outputs[field].at[:, pl.ds(tile * LANE, LANE)],
            sems.at[field, tile],
        )
        for field in range(FIELDS)
        for tile in range(fields_in.shape[1])
    ]
    copies.append(pltpu.make_async_copy(surface_in, surface_out, sems.at[FIELDS, 0]))
    for copy in copies:
        copy.start()
    for copy in copies:
        copy.wait()


def body(by_count, bx_count, u, v, t, s, wind, ssh, depth):
    levels, rows, cols = u.shape
    groups = -(-levels // SUB)
    span = rows + 2 * HALO
    room = span + 4
    tiles = cols // LANE
    width = cols + LANE
    f32 = jnp.float32
    flat_shape = (levels * rows, cols)
    args = [item.reshape(flat_shape) for item in (u, v, t, s)]
    own = jax.ShapeDtypeStruct((FIELDS, tiles, (groups + 1) * SUB * rows, LANE), f32)
    done, surface = pl.pallas_call(
        functools.partial(kernel, levels, rows * by_count, by_count, bx_count),
        out_shape=[own, jax.ShapeDtypeStruct(ssh.shape, f32)],
        in_specs=[pl.BlockSpec(memory_space=pltpu.HBM)] * (FIELDS + 3),
        out_specs=[pl.BlockSpec(memory_space=pltpu.VMEM)] * 2,
        scratch_shapes=[
            pltpu.VMEM((groups + 3, FIELDS, room, SUB, width), f32),
            pltpu.VMEM((rows, cols), jnp.int32),
            pltpu.VMEM((2, groups + 1, SUB, LANE), f32),
            pltpu.VMEM((2, groups + 1, SUB, LANE), f32),
            pltpu.VMEM((2, groups + 1, SUB, LANE), f32),
            pltpu.VMEM((2, groups + 1, SUB, LANE), f32),
            pltpu.VMEM((groups + 1, FIELDS, SUB, LANE), f32),
            pltpu.VMEM((FIELDS, room, SUB, width), f32),
            pltpu.VMEM((FIELDS, room, SUB, width), f32),
            pltpu.VMEM((2, room, SUB, width), f32),
            pltpu.VMEM((room, SUB, width), f32),
            pltpu.VMEM((room, SUB, width), f32),
            pltpu.VMEM((room, SUB, width), f32),
            pltpu.VMEM((2, room, SUB, width), f32),
            pltpu.VMEM((room, SUB, LANE), f32),
            pltpu.VMEM((2, rows, SUB, cols), f32),
            pltpu.VMEM((2, rows, cols), f32),
            pltpu.VMEM((2, 2, rows, cols), f32),
            pltpu.VMEM((2, 2, rows, LANE), f32),
            pltpu.VMEM((2, 2, 2, rows, LANE), f32),
            pltpu.VMEM((6, span, width), f32),
            pltpu.SemaphoreType.DMA((tiles, FIELDS + 3)),
            pltpu.SemaphoreType.DMA((2, groups + 1)),
            pltpu.SemaphoreType.DMA((2, groups + 1)),
            pltpu.SemaphoreType.DMA((2,)),
            pltpu.SemaphoreType.DMA((2,)),
            pltpu.SemaphoreType.DMA((2,)),
            pltpu.SemaphoreType.DMA((2,)),
            pltpu.SemaphoreType.DMA((8,)),
            pltpu.SemaphoreType.DMA((8,)),
        ],
        compiler_params=pltpu.CompilerParams(
            collective_id=0, has_side_effects=True, vmem_limit_bytes=61 << 20
        ),
    )(*args, wind.reshape(2 * rows, cols), ssh, depth)
    outs = pl.pallas_call(
        functools.partial(deliver, levels),
        out_shape=[jax.ShapeDtypeStruct(flat_shape, f32)] * FIELDS + [jax.ShapeDtypeStruct(ssh.shape, f32)],
        in_specs=[pl.BlockSpec(memory_space=pltpu.VMEM)] * 2,
        out_specs=[pl.BlockSpec(memory_space=pltpu.HBM)] * (FIELDS + 1),
        scratch_shapes=[pltpu.SemaphoreType.DMA((FIELDS + 1, tiles))],
    )(done, surface)
    return tuple(item.reshape(u.shape) for item in outs[:FIELDS]) + (outs[FIELDS],)


def solution(mesh):
    whole = P(None, "by", "bx")
    flat = P("by", "bx")
    return jax.shard_map(
        functools.partial(body, mesh.shape["by"], mesh.shape["bx"]),
        mesh=mesh,
        in_specs=(whole,) * 5 + (flat, flat),
        out_specs=(whole,) * 4 + (flat,),
        check_vma=False,
    )
```

```python
import functools
import math

import jax
import jax.numpy as jnp
from jax import lax
from jax.experimental import pallas as pl
from jax.experimental.pallas import tpu as pltpu
from jax.sharding import PartitionSpec as P

ITERS = 4
KAPPA = 0.004
ADVECT = 0.25
PRESS = 0.1
WIND = 0.5
PHI = 0.5
DIVERGE = 2.0
LOWER = 0.2
UPPER = 2.0

MESH = pl.DeviceIdType.MESH
FIELDS = 4
HALO = 4
SUB = 8
LANE = 128
BATCH = 3
FIRST = 5
SECOND = 4
FINISH = 8


def chebyshev_weights(count):
    middle = 0.5 * (UPPER + LOWER)
    half_span = 0.5 * (UPPER - LOWER)
    ratio_value = middle / half_span
    rho_now = 1.0 / ratio_value
    updates = []
    for _ in range(count - 1):
        rho_next = 1.0 / (2.0 * ratio_value - rho_now)
        updates.append((rho_next * rho_now, 2.0 * rho_next / half_span))
        rho_now = rho_next
    return 1.0 / middle, updates


def east(x):
    return pltpu.roll(x, x.shape[1] - 1, 1)


def west(x):
    return pltpu.roll(x, 1, 1)


def north(x):
    return pltpu.roll(x, x.shape[0] - 1, 0)


def south(x):
    return pltpu.roll(x, 1, 0)


def slot_lane(field, row):
    return (field % 2) * 64 + row * 8 + (field // 2) * 4


def turn(x, shift):
    shift = shift % LANE
    return x if shift == 0 else pltpu.roll(x, shift, 1)


def kernel(
    levels, total_rows, by_count, bx_count,
    u_in, v_in, t_in, s_in, wind_in, ssh_in, depth_in,
    own, surface_out,
    ext, depth_own, pack_send, pack_recv,
    lap, mix, press, depth_c, depth_e, depth_n, stress, cor,
    flow_sum, moved, moved_rows, moved_cols, moved_corners, flat,
    in_sem, row_send, row_recv, pack_ss, pack_rs, moved_ss, moved_rs,
):
    inputs = (u_in, v_in, t_in, s_in)
    rows = SUB
    span = rows + 2 * HALO
    width = ext.shape[-1]
    cols = width - LANE
    tiles = cols // LANE
    groups = -(-levels // SUB)
    block = SUB * rows
    base = groups * block
    by = lax.axis_index("by")
    bx = lax.axis_index("bx")

    def device(step_y, step_x):
        return (lax.rem(by + step_y + by_count, by_count), lax.rem(bx + step_x + bx_count, bx_count))

    neighbours = [(y, x) for y in (-1, 0, 1) for x in (-1, 0, 1) if (y, x) != (0, 0)]

    def load_copies():
        result = []
        for tile in range(tiles):
            lanes = pl.ds(tile * LANE, LANE)
            for field in range(FIELDS):
                result.append(pltpu.make_async_copy(
                    inputs[field].at[:, lanes], own.at[field, tile, pl.ds(0, levels * rows)], in_sem.at[tile, field]
                ))
            result.append(pltpu.make_async_copy(
                ssh_in.at[:, lanes], own.at[0, tile, pl.ds(base + rows, rows)], in_sem.at[tile, FIELDS]
            ))
            result.append(pltpu.make_async_copy(
                wind_in.at[:, lanes], own.at[0, tile, pl.ds(base + 2 * rows, 2 * rows)], in_sem.at[tile, FIELDS + 1]
            ))
        result.append(pltpu.make_async_copy(depth_in, depth_own, in_sem.at[0, FIELDS + 2]))
        return result

    for copy in load_copies():
        copy.start()

    barrier = pltpu.get_barrier_semaphore()
    for step in neighbours:
        pl.semaphore_signal(barrier, inc=1, device_id=device(*step), device_id_type=MESH)

    lane = lax.broadcasted_iota(jnp.int32, (SUB, LANE), 1)
    for tile in range(tiles):
        for field in range(FIELDS):
            if levels % SUB:
                pad = base - levels * rows
                own[field, tile, levels * rows : base, :] = jnp.zeros((pad, LANE), jnp.float32)
        own[0, tile, base + 4 * rows : base + block, :] = jnp.zeros((block - 4 * rows, LANE), jnp.float32)

    def row_copy(group, fields, side):
        source = HALO + rows - HALO if side == 0 else HALO
        target = 0 if side == 0 else HALO + rows
        return pltpu.make_async_remote_copy(
            src_ref=ext.at[group, pl.ds(0, fields), pl.ds(source, HALO), :, pl.ds(0, cols)],
            dst_ref=ext.at[group, pl.ds(0, fields), pl.ds(target, HALO), :, pl.ds(0, cols)],
            send_sem=row_send.at[side, group],
            recv_sem=row_recv.at[side, group],
            device_id=device(1 - 2 * side, 0),
            device_id_type=MESH,
        )

    batches = ((0, BATCH), (BATCH, groups + 1 - BATCH))

    def pack_copy(batch, y, x):
        first, count = batches[batch]
        place = 2 * (y % 3) + (1 - x) // 2
        return pltpu.make_async_remote_copy(
            src_ref=pack_send.at[(1 + x) // 2, pl.ds(first, count)],
            dst_ref=pack_recv.at[y % 3, (1 - x) // 2, pl.ds(first, count)],
            send_sem=pack_ss.at[batch, place],
            recv_sem=pack_rs.at[batch, place],
            device_id=device(y, x),
            device_id_type=MESH,
        )

    sideways = [(y, x) for y in (0, 1, -1) for x in (-1, 1)]

    def group_of(index):
        return lax.rem(index + groups, groups + 1)

    for copy in load_copies():
        copy.wait()
    for tile in range(tiles):
        own[0, tile, base : base + rows, :] = depth_own[:, tile * LANE : (tile + 1) * LANE].astype(jnp.float32)
    pl.semaphore_wait(barrier, len(neighbours))

    def stage_step(index, carry):
        group = group_of(index)
        west_pack = jnp.zeros((SUB, LANE), jnp.float32)
        east_pack = jnp.zeros((SUB, LANE), jnp.float32)
        for field in range(FIELDS):
            for row in range(rows):
                parts = [
                    own[field, tile, pl.ds(group * block + row, SUB, stride=rows), :]
                    for tile in range(tiles)
                ]
                for tile in range(tiles):
                    ext[group, field, HALO + row, :, tile * LANE : (tile + 1) * LANE] = parts[tile]
                first = slot_lane(field, row)
                here = (lane >= first) & (lane < first + HALO)
                west_pack = jnp.where(here, turn(parts[0], first), west_pack)
                east_pack = jnp.where(here, turn(parts[-1], first + HALO), east_pack)
        pack_send[0, index] = west_pack
        pack_send[1, index] = east_pack

        return carry

    assert (groups + 1) % BATCH == 0

    def stage_batch(index, carry):
        for k in range(BATCH):
            stage_step(index * BATCH + k, 0)

        @pl.when(index == 0)
        def _():
            for side in range(2):
                row_copy(groups, 1, side).start()
            for step in sideways:
                pack_copy(0, *step).start()
            for group in range(BATCH - 1):
                for side in range(2):
                    row_copy(group, FIELDS, side).start()

        return carry

    lax.fori_loop(0, (groups + 1) // BATCH, stage_batch, 0)
    for step in sideways:
        pack_copy(1, *step).start()

    def send_step(group, carry):
        for side in range(2):
            row_copy(group, FIELDS, side).start()
        return carry

    lax.fori_loop(BATCH - 1, groups, send_step, 0)

    row_index = by * rows - HALO + lax.broadcasted_iota(jnp.int32, (span, LANE), 0)
    turning = 1.2 * jnp.sin(0.9 * math.pi * ((row_index.astype(jnp.float32) + 0.5) / total_rows - 0.5))
    for row in range(span):
        cor[row] = jnp.broadcast_to(turning[row : row + 1, :], (SUB, LANE))

    sub = lax.broadcasted_iota(jnp.int32, (SUB, width), 0)
    level = sub.astype(jnp.float32)
    zeros = jnp.zeros((SUB, width), jnp.float32)

    for row in range(span):
        press[0, row] = zeros
        press[1, row] = zeros
    for axis in range(2):
        for row in range(rows):
            flow_sum[axis, row] = jnp.zeros((SUB, cols), jnp.float32)

    def operator(field, corner):
        north_field = north(field)
        total = field + north_field
        change = north_field - field
        flux_x = corner * (0.5 * (east(total) - total))
        flux_y = corner * (0.5 * (east(change) + change))
        along_x = flux_x + south(flux_x)
        along_y = flux_y + west(flux_y)
        return PHI * field - 0.5 * ((along_x - west(along_x)) + (along_y - south(along_y)))

    def flat_tables():
        for row in range(span):
            index = by * rows + (row - HALO)
            inside = (index >= 0) & (index < total_rows)
            here = jnp.where(inside, jnp.broadcast_to(ext[groups, 0, row, 0:1, :], (SUB, width)), 0.0)
            depth_c[row] = here
            depth_e[row] = jnp.minimum(here, east(here))
            if row > 0:
                depth_n[row - 1] = jnp.minimum(before, here)
            before = here
            for axis in range(2):
                wind = jnp.broadcast_to(ext[groups, 0, row, 2 + axis : 3 + axis, :], (SUB, width))
                stress[axis, row] = jnp.where(sub == 0, WIND * wind, 0.0)
            place = (row + span - HALO) % span
            flat[0, place : place + 1, :] = here[0:1, :]
            flat[1, place : place + 1, :] = ext[groups, 0, row, 1:2, :]
        depth = flat[0]
        ssh = flat[1]
        near = jnp.minimum(depth, east(depth))
        corner = jnp.minimum(near, north(near)) * (1.0 / levels)
        pair = corner + west(corner)
        ocean = jnp.where(depth > 0.0, 1.0, 0.0)
        flat[2] = corner
        flat[3] = 1.0 / (PHI + 0.5 * (pair + south(pair)))
        flat[4] = ocean
        flat[5] = ocean * (PHI * ssh) - operator(ssh, corner)

    def cut(mask, value):
        return jnp.where(mask, value, 0.0)

    def tendencies(group):
        number = level + (group * SUB).astype(jnp.float32)

        def stage_pass(part, carry):
            slot = jnp.where(part == 0, group, groups + part)
            after = groups + 1 + part

            def first_block(index, inner):
                row = 1 + 2 * part + index * FIRST
                wet = [number < depth_c[row + k] for k in range(FIRST)]
                wet_e = [number < depth_e[row + k] for k in range(FIRST)]
                wet_n = [number < depth_n[row - 1 + k] for k in range(FIRST + 1)]
                speed = [
                    [(-0.5 * ADVECT) * ext[slot, field, row + k] for field in range(2)] for k in range(FIRST)
                ]
                for field in range(FIELDS):
                    cells = [ext[slot, field, row - 1 + k] for k in range(FIRST + 2)]
                    faces = [cut(wet_n[k], cells[k + 1] - cells[k]) for k in range(FIRST + 1)]
                    for k in range(FIRST):
                        here = cells[k + 1]
                        face_e = cut(wet_e[k], east(here) - here)
                        face_w = west(face_e)
                        lap[field, row + k] = (face_e - face_w) + (faces[k + 1] - faces[k])
                        mix[field, row + k] = speed[k][0] * (face_e + face_w) + speed[k][1] * (
                            faces[k + 1] + faces[k]
                        )
                above = [
                    jnp.broadcast_to(press[part, row + k, SUB - 1 : SUB, :], (SUB, width)) for k in range(FIRST)
                ]
                for k in range(FIRST):
                    running = cut(
                        wet[k],
                        (-0.8 * PRESS) * ext[slot, 2, row + k] + (0.6 * PRESS) * ext[slot, 3, row + k],
                    )
                    for shift in (1, 2, 4):
                        running = running + jnp.where(sub >= shift, pltpu.roll(running, shift, 0), 0.0)
                    press[part, row + k] = above[k] + running
                return inner

            def second_block(index, inner):
                row = 2 + 2 * part + index * SECOND
                wet = [number < depth_c[row + k] for k in range(SECOND)]
                wet_e = [number < depth_e[row + k] for k in range(SECOND)]
                wet_n = [number < depth_n[row - 1 + k] for k in range(SECOND + 1)]
                cells = [press[part, row - 1 + k] for k in range(SECOND + 2)]
                faces = [cut(wet_n[k], cells[k + 1] - cells[k]) for k in range(SECOND + 1)]
                forced = []
                for k in range(SECOND):
                    here = cells[k + 1]
                    face_e = cut(wet_e[k], east(here) - here)
                    turned = jnp.concatenate([cor[row + k]] * (width // LANE), axis=1)
                    forced.append((
                        cut(wet[k], turned * ext[slot, 1, row + k]) - 0.5 * (face_e + west(face_e)),
                        cut(wet[k], -turned * ext[slot, 0, row + k]) - 0.5 * (faces[k + 1] + faces[k]),
                    ))
                results = []
                for field in range(FIELDS):
                    cells = [lap[field, row - 1 + k] for k in range(SECOND + 2)]
                    faces = [cut(wet_n[k], cells[k + 1] - cells[k]) for k in range(SECOND + 1)]
                    for k in range(SECOND):
                        here = cells[k + 1]
                        face_e = cut(wet_e[k], east(here) - here)
                        twice = (face_e - west(face_e)) + (faces[k + 1] - faces[k])
                        value = (ext[slot, field, row + k] + mix[field, row + k]) - KAPPA * twice
                        results.append((field, row + k, value + forced[k][field] if field < 2 else value))
                for field, place, value in results:
                    ext[after, field, place] = value
                return inner

            lax.fori_loop(0, (span - 2 - 4 * part + FIRST - 1) // FIRST, first_block, 0)
            lax.fori_loop(0, (span - 4 - 4 * part + SECOND - 1) // SECOND, second_block, 0)
            @pl.when(group == 0)
            def _():
                for row in range(2, span - 2):
                    for axis in range(2):
                        ext[after, axis, row] = ext[after, axis, row] + cut(number < depth_c[row], stress[axis, row])

            return carry

        lax.fori_loop(0, 2, stage_pass, 0)

        def finish_block(index, carry):
            for k in range(FINISH):
                row = index * FINISH + k
                wet = (number < depth_c[row + HALO])[:, :cols]
                for field in range(FIELDS):
                    value = 0.5 * (
                        ext[group, field, row + HALO, :, :cols] + ext[groups + 2, field, row + HALO, :, :cols]
                    )
                    for tile in range(tiles):
                        own[field, tile, pl.ds(group * block + row, SUB, stride=rows), :] = value[
                            :, tile * LANE : (tile + 1) * LANE
                        ]
                    if field < 2:
                        flow_sum[field, row] = flow_sum[field, row] + cut(wet, value)
            return carry

        lax.fori_loop(0, rows // FINISH, finish_block, 0)

    west_lanes = (lane & 7) < HALO

    def widen(index, group, fields):
        packs = [[pack_recv[y, x, index] for x in range(2)] for y in range(3)]
        for field in range(fields):
            shifts = (
                HALO * 8 - slot_lane(field, 0), -slot_lane(field, rows - HALO), (HALO + rows) * 8 - slot_lane(field, 0)
            )
            parts = [
                jnp.where(west_lanes, turn(packs[y][0], shifts[y]), turn(packs[y][1], shifts[y] + HALO))
                for y in range(3)
            ]
            all_rows = jnp.where(
                lane < HALO * 8, parts[1], jnp.where(lane < (HALO + rows) * 8, parts[0], parts[2])
            )
            for row in range(span):
                ext[group, field, row, :, cols:width] = turn(all_rows, LANE - HALO - 8 * row)

    for step in sideways:
        pack_copy(0, *step).wait_recv()
    for side in range(2):
        row_copy(groups, 1, side).wait_recv()
    widen(0, groups, 1)
    flat_tables()

    def group_step(group, carry):
        for side in range(2):
            row_copy(group, FIELDS, side).wait_recv()

        @pl.when(group == BATCH - 1)
        def _():
            for step in sideways:
                pack_copy(1, *step).wait_recv()

        widen(group + 1, group, FIELDS)
        tendencies(group)
        return carry

    lax.fori_loop(0, groups, group_step, 0)

    for row in range(rows):
        for axis in range(2):
            total = jnp.sum(flow_sum[axis, row], axis=0, keepdims=True) * (1.0 / levels)
            moved[axis, row : row + 1, :] = total

    def moved_copy(step):
        y, x = step
        place = neighbours.index(step)
        other = neighbours.index((-y, -x))
        if x == 0:
            source, target = moved, moved_rows.at[(1 - y) // 2]
        else:
            tile = tiles - 1 if x > 0 else 0
            source = moved.at[:, :, pl.ds(tile * LANE, LANE)]
            side = (1 - x) // 2
            target = moved_cols.at[side] if y == 0 else moved_corners.at[(1 - y) // 2, side]
        return pltpu.make_async_remote_copy(
            src_ref=source, dst_ref=target, send_sem=moved_ss.at[place], recv_sem=moved_rs.at[place],
            device_id=device(y, x), device_id_type=MESH,
        )

    for step in neighbours:
        moved_copy(step).start()
    for step in neighbours:
        moved_copy(step).wait_recv()
    lower = lax.broadcasted_iota(jnp.int32, (SUB, cols), 0) < HALO
    lower_tile = lax.broadcasted_iota(jnp.int32, (SUB, LANE), 0) < HALO
    right = lane < LANE // 2
    transports = []
    for axis in range(2):
        near = jnp.concatenate(
            [moved[axis], jnp.where(right, moved_cols[1, axis], moved_cols[0, axis])], axis=1
        )
        corners = [
            jnp.where(right, moved_corners[side, 1, axis], moved_corners[side, 0, axis]) for side in range(2)
        ]
        far = jnp.concatenate(
            [
                jnp.where(lower, moved_rows[1, axis], moved_rows[0, axis]),
                jnp.where(lower_tile, corners[1], corners[0]),
            ],
            axis=1,
        )
        transports.append(jnp.concatenate([near, far], axis=0))

    corner = flat[2]
    diagonal_inverse = flat[3]
    ocean = flat[4]
    face_x = ocean * east(ocean) * (east(transports[0]) - transports[0])
    face_y = ocean * north(ocean) * (north(transports[1]) - transports[1])
    spread = 0.5 * ((face_x + west(face_x)) + (face_y + south(face_y)))
    residual = flat[5] - (DIVERGE * ocean) * spread
    opening, updates = chebyshev_weights(ITERS)
    direction = opening * (residual * diagonal_inverse)

    def pick(index, values):
        result = jnp.float32(values[-1])
        for k in range(len(values) - 1):
            result = jnp.where(index == k, jnp.float32(values[k]), result)
        return result

    def solve_step(index, carry):
        surface, residual, direction = carry
        surface = surface + direction
        residual = residual - operator(direction, corner)
        keep = pick(index, [item[0] for item in updates])
        push = pick(index, [item[1] for item in updates])
        direction = keep * direction + push * (residual * diagonal_inverse)
        return surface, residual, direction

    surface, residual, direction = lax.fori_loop(0, ITERS - 1, solve_step, (flat[1], residual, direction))
    surface_out[...] = (surface + direction)[:rows, :cols]

    for side in range(2):
        row_copy(groups, 1, side).wait_send()
    for step in neighbours:
        moved_copy(step).wait_send()
    for step in sideways:
        for batch in range(2):
            pack_copy(batch, *step).wait_send()

    def drain(group, carry):
        for side in range(2):
            row_copy(group, FIELDS, side).wait_send()
        return carry

    lax.fori_loop(0, groups, drain, 0)


def deliver(levels, fields_in, surface_in, u_out, v_out, t_out, s_out, surface_out, sems):
    outputs = (u_out, v_out, t_out, s_out)
    count = u_out.shape[0]
    copies = [
        pltpu.make_async_copy(
            fields_in.at[field, tile, pl.ds(0, count)],
            outputs[field].at[:, pl.ds(tile * LANE, LANE)],
            sems.at[field, tile],
        )
        for field in range(FIELDS)
        for tile in range(fields_in.shape[1])
    ]
    copies.append(pltpu.make_async_copy(surface_in, surface_out, sems.at[FIELDS, 0]))
    for copy in copies:
        copy.start()
    for copy in copies:
        copy.wait()


def body(by_count, bx_count, u, v, t, s, wind, ssh, depth):
    levels, rows, cols = u.shape
    groups = -(-levels // SUB)
    span = rows + 2 * HALO
    room = span + 4
    tiles = cols // LANE
    width = cols + LANE
    f32 = jnp.float32
    flat_shape = (levels * rows, cols)
    args = [item.reshape(flat_shape) for item in (u, v, t, s)]
    own = jax.ShapeDtypeStruct((FIELDS, tiles, (groups + 1) * SUB * rows, LANE), f32)
    done, surface = pl.pallas_call(
        functools.partial(kernel, levels, rows * by_count, by_count, bx_count),
        out_shape=[pltpu.VMEM(own.shape, f32), pltpu.VMEM(ssh.shape, f32)],
        in_specs=[pl.BlockSpec(memory_space=pltpu.HBM)] * (FIELDS + 3),
        out_specs=[pl.BlockSpec(memory_space=pltpu.VMEM)] * 2,
        scratch_shapes=[
            pltpu.VMEM((groups + 3, FIELDS, room, SUB, width), f32),
            pltpu.VMEM((rows, cols), jnp.int32),
            pltpu.VMEM((2, groups + 1, SUB, LANE), f32),
            pltpu.VMEM((3, 2, groups + 1, SUB, LANE), f32),
            pltpu.VMEM((FIELDS, room, SUB, width), f32),
            pltpu.VMEM((FIELDS, room, SUB, width), f32),
            pltpu.VMEM((2, room, SUB, width), f32),
            pltpu.VMEM((room, SUB, width), f32),
            pltpu.VMEM((room, SUB, width), f32),
            pltpu.VMEM((room, SUB, width), f32),
            pltpu.VMEM((2, room, SUB, width), f32),
            pltpu.VMEM((room, SUB, LANE), f32),
            pltpu.VMEM((2, rows, SUB, cols), f32),
            pltpu.VMEM((2, rows, cols), f32),
            pltpu.VMEM((2, 2, rows, cols), f32),
            pltpu.VMEM((2, 2, rows, LANE), f32),
            pltpu.VMEM((2, 2, 2, rows, LANE), f32),
            pltpu.VMEM((6, span, width), f32),
            pltpu.SemaphoreType.DMA((tiles, FIELDS + 3)),
            pltpu.SemaphoreType.DMA((2, groups + 1)),
            pltpu.SemaphoreType.DMA((2, groups + 1)),
            pltpu.SemaphoreType.DMA((2, 6)),
            pltpu.SemaphoreType.DMA((2, 6)),
            pltpu.SemaphoreType.DMA((8,)),
            pltpu.SemaphoreType.DMA((8,)),
        ],
        compiler_params=pltpu.CompilerParams(
            collective_id=0, has_side_effects=True, vmem_limit_bytes=61 << 20
        ),
    )(*args, wind.reshape(2 * rows, cols), ssh, depth)
    outs = pl.pallas_call(
        functools.partial(deliver, levels),
        out_shape=[jax.ShapeDtypeStruct(flat_shape, f32)] * FIELDS + [jax.ShapeDtypeStruct(ssh.shape, f32)],
        in_specs=[pl.BlockSpec(memory_space=pltpu.VMEM)] * 2,
        out_specs=[pl.BlockSpec(memory_space=pltpu.HBM)] * (FIELDS + 1),
        scratch_shapes=[pltpu.SemaphoreType.DMA((FIELDS + 1, tiles))],
        compiler_params=pltpu.CompilerParams(vmem_limit_bytes=4 << 20),
    )(done, surface)
    return tuple(item.reshape(u.shape) for item in outs[:FIELDS]) + (outs[FIELDS],)


def solution(mesh):
    whole = P(None, "by", "bx")
    flat = P("by", "bx")
    return jax.shard_map(
        functools.partial(body, mesh.shape["by"], mesh.shape["bx"]),
        mesh=mesh,
        in_specs=(whole,) * 5 + (flat, flat),
        out_specs=(whole,) * 4 + (flat,),
        check_vma=False,
    )
```

```python
import functools
import math

import jax
import jax.numpy as jnp
from jax import lax
from jax.experimental import pallas as pl
from jax.experimental.pallas import tpu as pltpu
from jax.sharding import PartitionSpec as P

ITERS = 4
KAPPA = 0.004
ADVECT = 0.25
PRESS = 0.1
WIND = 0.5
PHI = 0.5
DIVERGE = 2.0
LOWER = 0.2
UPPER = 2.0

MESH = pl.DeviceIdType.MESH
FIELDS = 4
HALO = 4
SUB = 8
LANE = 128
BATCH = 4
FIRST = 5
SECOND = 4


def chebyshev_weights(count):
    middle = 0.5 * (UPPER + LOWER)
    half_span = 0.5 * (UPPER - LOWER)
    ratio_value = middle / half_span
    rho_now = 1.0 / ratio_value
    updates = []
    for _ in range(count - 1):
        rho_next = 1.0 / (2.0 * ratio_value - rho_now)
        updates.append((rho_next * rho_now, 2.0 * rho_next / half_span))
        rho_now = rho_next
    return 1.0 / middle, updates


def east(x):
    return pltpu.roll(x, x.shape[1] - 1, 1)


def west(x):
    return pltpu.roll(x, 1, 1)


def north(x):
    return pltpu.roll(x, x.shape[0] - 1, 0)


def south(x):
    return pltpu.roll(x, 1, 0)


def slot_lane(field, row):
    return (field % 2) * 64 + row * 8 + (field // 2) * 4


def turn(x, shift):
    shift = shift % LANE
    return x if shift == 0 else pltpu.roll(x, shift, 1)


def kernel(
    levels, total_rows, by_count, bx_count,
    u_in, v_in, t_in, s_in, wind_in, ssh_in, depth_in,
    own, surface_out,
    ext, depth_own, pack_send, pack_recv,
    lap, mix, press, depth_c, depth_e, depth_n, stress, cor,
    flow_sum, moved, moved_rows, moved_cols, moved_corners, flat,
    in_sem, row_send, row_recv, pack_ss, pack_rs, moved_ss, moved_rs,
):
    inputs = (u_in, v_in, t_in, s_in)
    rows = SUB
    span = rows + 2 * HALO
    width = ext.shape[-1]
    cols = width - LANE
    tiles = cols // LANE
    groups = -(-levels // SUB)
    block = SUB * rows
    lead = groups * SUB - levels
    assert lead >= 2
    by = lax.axis_index("by")
    bx = lax.axis_index("bx")

    def device(step_y, step_x):
        return (lax.rem(by + step_y + by_count, by_count), lax.rem(bx + step_x + bx_count, bx_count))

    neighbours = [(y, x) for y in (-1, 0, 1) for x in (-1, 0, 1) if (y, x) != (0, 0)]

    def load_copies():
        result = []
        for tile in range(tiles):
            lanes = pl.ds(tile * LANE, LANE)
            for field in range(FIELDS):
                result.append(pltpu.make_async_copy(
                    inputs[field].at[:, lanes], own.at[field, tile, pl.ds(lead * rows, levels * rows)], in_sem.at[tile, field]
                ))
            result.append(pltpu.make_async_copy(
                ssh_in.at[:, lanes], own.at[0, tile, pl.ds(rows, rows)], in_sem.at[tile, FIELDS]
            ))
            result.append(pltpu.make_async_copy(
                wind_in.at[:, lanes], own.at[1, tile, pl.ds(0, 2 * rows)], in_sem.at[tile, FIELDS + 1]
            ))
        result.append(pltpu.make_async_copy(depth_in, depth_own, in_sem.at[0, FIELDS + 2]))
        return result

    for copy in load_copies():
        copy.start()

    barrier = pltpu.get_barrier_semaphore()
    for step in neighbours:
        pl.semaphore_signal(barrier, inc=1, device_id=device(*step), device_id_type=MESH)

    lane = lax.broadcasted_iota(jnp.int32, (SUB, LANE), 1)
    for tile in range(tiles):
        for field in range(2, FIELDS):
            own[field, tile, : lead * rows, :] = jnp.zeros((lead * rows, LANE), jnp.float32)
        if lead > 2:
            for field in range(2):
                own[field, tile, 2 * rows : lead * rows, :] = jnp.zeros(((lead - 2) * rows, LANE), jnp.float32)

    def row_copy(group, side):
        source = HALO + rows - HALO if side == 0 else HALO
        target = 0 if side == 0 else HALO + rows
        return pltpu.make_async_remote_copy(
            src_ref=ext.at[group, :, pl.ds(source, HALO), :, pl.ds(0, cols)],
            dst_ref=ext.at[group, :, pl.ds(target, HALO), :, pl.ds(0, cols)],
            send_sem=row_send.at[side, group],
            recv_sem=row_recv.at[side, group],
            device_id=device(1 - 2 * side, 0),
            device_id_type=MESH,
        )

    batches = ((0, BATCH), (BATCH, groups - BATCH))

    def pack_copy(batch, y, x):
        first, count = batches[batch]
        place = 2 * (y % 3) + (1 - x) // 2
        return pltpu.make_async_remote_copy(
            src_ref=pack_send.at[(1 + x) // 2, pl.ds(first, count)],
            dst_ref=pack_recv.at[y % 3, (1 - x) // 2, pl.ds(first, count)],
            send_sem=pack_ss.at[batch, place],
            recv_sem=pack_rs.at[batch, place],
            device_id=device(y, x),
            device_id_type=MESH,
        )

    sideways = [(y, x) for y in (0, 1, -1) for x in (-1, 1)]

    for copy in load_copies():
        copy.wait()
    for tile in range(tiles):
        own[0, tile, :rows, :] = depth_own[:, tile * LANE : (tile + 1) * LANE].astype(jnp.float32)
    pl.semaphore_wait(barrier, len(neighbours))

    def stage_step(group):
        west_pack = jnp.zeros((SUB, LANE), jnp.float32)
        east_pack = jnp.zeros((SUB, LANE), jnp.float32)
        for field in range(FIELDS):
            for row in range(rows):
                parts = [
                    own[field, tile, pl.ds(group * block + row, SUB, stride=rows), :]
                    for tile in range(tiles)
                ]
                for tile in range(tiles):
                    ext[group, field, HALO + row, :, tile * LANE : (tile + 1) * LANE] = parts[tile]
                first = slot_lane(field, row)
                here = (lane >= first) & (lane < first + HALO)
                west_pack = jnp.where(here, turn(parts[0], first), west_pack)
                east_pack = jnp.where(here, turn(parts[-1], first + HALO), east_pack)
        pack_send[0, group] = west_pack
        pack_send[1, group] = east_pack

    assert groups % BATCH == 0

    def stage_batch(index, carry):
        for k in range(BATCH):
            stage_step(index * BATCH + k)

        @pl.when(index == 0)
        def _():
            for side in range(2):
                row_copy(0, side).start()
            for step in sideways:
                pack_copy(0, *step).start()
            for group in range(1, BATCH):
                for side in range(2):
                    row_copy(group, side).start()

        return carry

    lax.fori_loop(0, groups // BATCH, stage_batch, 0)
    for step in sideways:
        pack_copy(1, *step).start()

    def send_step(group, carry):
        for side in range(2):
            row_copy(group, side).start()
        return carry

    lax.fori_loop(BATCH, groups, send_step, 0)

    row_index = by * rows - HALO + lax.broadcasted_iota(jnp.int32, (span, LANE), 0)
    turning = 1.2 * jnp.sin(0.9 * math.pi * ((row_index.astype(jnp.float32) + 0.5) / total_rows - 0.5))
    for row in range(span):
        cor[row] = jnp.broadcast_to(turning[row : row + 1, :], (SUB, LANE))

    sub = lax.broadcasted_iota(jnp.int32, (SUB, width), 0)
    level = sub.astype(jnp.float32)
    zeros = jnp.zeros((SUB, width), jnp.float32)

    for row in range(span):
        press[0, row] = zeros
        press[1, row] = zeros
    for axis in range(2):
        for row in range(rows):
            flow_sum[axis, row] = jnp.zeros((SUB, cols), jnp.float32)

    def operator(field, corner):
        north_field = north(field)
        total = field + north_field
        change = north_field - field
        flux_x = corner * (0.5 * (east(total) - total))
        flux_y = corner * (0.5 * (east(change) + change))
        along_x = flux_x + south(flux_x)
        along_y = flux_y + west(flux_y)
        return PHI * field - 0.5 * ((along_x - west(along_x)) + (along_y - south(along_y)))

    def flat_tables():
        for row in range(span):
            index = by * rows + (row - HALO)
            inside = (index >= 0) & (index < total_rows)
            here = jnp.where(inside, jnp.broadcast_to(ext[0, 0, row, 0:1, :], (SUB, width)), 0.0)
            depth_c[row] = here
            depth_e[row] = jnp.minimum(here, east(here))
            if row > 0:
                depth_n[row - 1] = jnp.minimum(before, here)
            before = here
            for axis in range(2):
                wind = jnp.broadcast_to(ext[0, 1, row, axis : axis + 1, :], (SUB, width))
                stress[axis, row] = jnp.where(sub == lead, WIND * wind, 0.0)
            place = (row + span - HALO) % span
            flat[0, place : place + 1, :] = here[0:1, :]
            flat[1, place : place + 1, :] = ext[0, 0, row, 1:2, :]
        depth = flat[0]
        ssh = flat[1]
        near = jnp.minimum(depth, east(depth))
        corner = jnp.minimum(near, north(near)) * (1.0 / levels)
        pair = corner + west(corner)
        ocean = jnp.where(depth > 0.0, 1.0, 0.0)
        flat[2] = corner
        flat[3] = 1.0 / (PHI + 0.5 * (pair + south(pair)))
        flat[4] = ocean
        flat[5] = ocean * (PHI * ssh) - operator(ssh, corner)

    def cut(mask, value):
        return jnp.where(mask, value, 0.0)

    def tendencies(group):
        number = level + (group * SUB - lead).astype(jnp.float32)
        number = jnp.where(number < 0.0, 1e9, number)

        def stage_pass(part):
            slot = group if part == 0 else groups
            keep = width if part == 0 else cols

            def first_block(index, inner):
                row = 1 + 2 * part + index * FIRST
                wet = [number < depth_c[row + k] for k in range(FIRST)]
                wet_e = [number < depth_e[row + k] for k in range(FIRST)]
                wet_n = [number < depth_n[row - 1 + k] for k in range(FIRST + 1)]
                speed = [
                    [(-0.5 * ADVECT) * ext[slot, field, row + k] for field in range(2)] for k in range(FIRST)
                ]
                for field in range(FIELDS):
                    cells = [ext[slot, field, row - 1 + k] for k in range(FIRST + 2)]
                    faces = [cut(wet_n[k], cells[k + 1] - cells[k]) for k in range(FIRST + 1)]
                    for k in range(FIRST):
                        here = cells[k + 1]
                        face_e = cut(wet_e[k], east(here) - here)
                        face_w = west(face_e)
                        lap[field, row + k] = (face_e - face_w) + (faces[k + 1] - faces[k])
                        mix[field, row + k] = speed[k][0] * (face_e + face_w) + speed[k][1] * (
                            faces[k + 1] + faces[k]
                        )
                above = [
                    jnp.broadcast_to(press[part, row + k, SUB - 1 : SUB, :], (SUB, width)) for k in range(FIRST)
                ]
                for k in range(FIRST):
                    running = cut(
                        wet[k],
                        (-0.8 * PRESS) * ext[slot, 2, row + k] + (0.6 * PRESS) * ext[slot, 3, row + k],
                    )
                    for shift in (1, 2, 4):
                        running = running + jnp.where(sub >= shift, pltpu.roll(running, shift, 0), 0.0)
                    press[part, row + k] = above[k] + running
                return inner

            def second_block(index, inner):
                row = 2 + 2 * part + index * SECOND
                wet = [(number < depth_c[row + k])[:, :keep] for k in range(SECOND)]
                wet_e = [number < depth_e[row + k] for k in range(SECOND)]
                wet_n = [(number < depth_n[row - 1 + k])[:, :keep] for k in range(SECOND + 1)]

                def differences(cells):
                    faces = [
                        cut(wet_n[k], cells[k + 1][:, :keep] - cells[k][:, :keep]) for k in range(SECOND + 1)
                    ]
                    result = []
                    for k in range(SECOND):
                        here = cells[k + 1]
                        face_e = cut(wet_e[k], east(here) - here)
                        result.append((face_e[:, :keep], west(face_e)[:, :keep], faces[k + 1], faces[k]))
                    return result

                forced = []
                cells = [press[part, row - 1 + k] for k in range(SECOND + 2)]
                for k, (face_e, face_w, face_n, face_s) in enumerate(differences(cells)):
                    turned = jnp.concatenate([cor[row + k]] * (keep // LANE), axis=1)
                    forced.append((
                        cut(wet[k], turned * ext[slot, 1, row + k, :, :keep]) - 0.5 * (face_e + face_w),
                        cut(wet[k], -turned * ext[slot, 0, row + k, :, :keep]) - 0.5 * (face_n + face_s),
                    ))
                results = []
                for field in range(FIELDS):
                    cells = [lap[field, row - 1 + k] for k in range(SECOND + 2)]
                    for k, (face_e, face_w, face_n, face_s) in enumerate(differences(cells)):
                        twice = (face_e - face_w) + (face_n - face_s)
                        value = (
                            ext[slot, field, row + k, :, :keep] + mix[field, row + k, :, :keep]
                        ) - KAPPA * twice
                        if field < 2:
                            value = value + forced[k][field]
                        if part == 1:
                            value = 0.5 * (ext[group, field, row + k, :, :keep] + value)
                        results.append((field, k, value))
                for field, k, value in results:
                    if part == 0:
                        ext[groups, field, row + k] = value
                        continue
                    inner_row = row + k - HALO
                    for tile in range(tiles):
                        own[field, tile, pl.ds(group * block + inner_row, SUB, stride=rows), :] = value[
                            :, tile * LANE : (tile + 1) * LANE
                        ]
                    if field < 2:
                        flow_sum[field, inner_row] = flow_sum[field, inner_row] + cut(wet[k], value)
                return inner

            lax.fori_loop(0, (span - 2 - 4 * part + FIRST - 1) // FIRST, first_block, 0)
            lax.fori_loop(0, (span - 4 - 4 * part + SECOND - 1) // SECOND, second_block, 0)

            @pl.when(group == 0)
            def _():
                for row in range(2 + 2 * part, span - 2 - 2 * part):
                    for axis in range(2):
                        wind = cut(number < depth_c[row], stress[axis, row])
                        if part == 0:
                            ext[groups, axis, row] = ext[groups, axis, row] + wind
                            continue
                        half = 0.5 * wind[:, :cols]
                        flow_sum[axis, row - HALO] = flow_sum[axis, row - HALO] + half
                        for tile in range(tiles):
                            place = pl.ds(row - HALO, SUB, stride=rows)
                            lanes = slice(tile * LANE, (tile + 1) * LANE)
                            own[axis, tile, place, :] = own[axis, tile, place, :] + half[:, lanes]

        stage_pass(0)
        stage_pass(1)

    west_lanes = (lane & 7) < HALO

    def widen(group):
        packs = [[pack_recv[y, x, group] for x in range(2)] for y in range(3)]
        for field in range(FIELDS):
            shifts = (
                HALO * 8 - slot_lane(field, 0), -slot_lane(field, rows - HALO), (HALO + rows) * 8 - slot_lane(field, 0)
            )
            parts = [
                jnp.where(west_lanes, turn(packs[y][0], shifts[y]), turn(packs[y][1], shifts[y] + HALO))
                for y in range(3)
            ]
            all_rows = jnp.where(
                lane < HALO * 8, parts[1], jnp.where(lane < (HALO + rows) * 8, parts[0], parts[2])
            )
            for row in range(span):
                ext[group, field, row, :, cols:width] = turn(all_rows, LANE - HALO - 8 * row)

    for step in sideways:
        pack_copy(0, *step).wait_recv()
    for side in range(2):
        row_copy(0, side).wait_recv()
    widen(0)
    flat_tables()

    def group_step(group, carry):
        @pl.when(group == BATCH)
        def _():
            for step in sideways:
                pack_copy(1, *step).wait_recv()

        @pl.when(group > 0)
        def _():
            for side in range(2):
                row_copy(group, side).wait_recv()
            widen(group)

        tendencies(group)
        return carry

    lax.fori_loop(0, groups, group_step, 0)

    for row in range(rows):
        for axis in range(2):
            total = jnp.sum(flow_sum[axis, row], axis=0, keepdims=True) * (1.0 / levels)
            moved[axis, row : row + 1, :] = total

    def moved_copy(step):
        y, x = step
        place = neighbours.index(step)
        other = neighbours.index((-y, -x))
        if x == 0:
            source, target = moved, moved_rows.at[(1 - y) // 2]
        else:
            tile = tiles - 1 if x > 0 else 0
            source = moved.at[:, :, pl.ds(tile * LANE, LANE)]
            side = (1 - x) // 2
            target = moved_cols.at[side] if y == 0 else moved_corners.at[(1 - y) // 2, side]
        return pltpu.make_async_remote_copy(
            src_ref=source, dst_ref=target, send_sem=moved_ss.at[place], recv_sem=moved_rs.at[place],
            device_id=device(y, x), device_id_type=MESH,
        )

    for step in neighbours:
        moved_copy(step).start()
    for step in neighbours:
        moved_copy(step).wait_recv()
    lower = lax.broadcasted_iota(jnp.int32, (SUB, cols), 0) < HALO
    lower_tile = lax.broadcasted_iota(jnp.int32, (SUB, LANE), 0) < HALO
    right = lane < LANE // 2
    transports = []
    for axis in range(2):
        near = jnp.concatenate(
            [moved[axis], jnp.where(right, moved_cols[1, axis], moved_cols[0, axis])], axis=1
        )
        corners = [
            jnp.where(right, moved_corners[side, 1, axis], moved_corners[side, 0, axis]) for side in range(2)
        ]
        far = jnp.concatenate(
            [
                jnp.where(lower, moved_rows[1, axis], moved_rows[0, axis]),
                jnp.where(lower_tile, corners[1], corners[0]),
            ],
            axis=1,
        )
        transports.append(jnp.concatenate([near, far], axis=0))

    corner = flat[2]
    diagonal_inverse = flat[3]
    ocean = flat[4]
    face_x = ocean * east(ocean) * (east(transports[0]) - transports[0])
    face_y = ocean * north(ocean) * (north(transports[1]) - transports[1])
    spread = 0.5 * ((face_x + west(face_x)) + (face_y + south(face_y)))
    residual = flat[5] - (DIVERGE * ocean) * spread
    opening, updates = chebyshev_weights(ITERS)
    direction = opening * (residual * diagonal_inverse)

    def pick(index, values):
        result = jnp.float32(values[-1])
        for k in range(len(values) - 1):
            result = jnp.where(index == k, jnp.float32(values[k]), result)
        return result

    def solve_step(index, carry):
        surface, residual, direction = carry
        surface = surface + direction
        residual = residual - operator(direction, corner)
        keep = pick(index, [item[0] for item in updates])
        push = pick(index, [item[1] for item in updates])
        direction = keep * direction + push * (residual * diagonal_inverse)
        return surface, residual, direction

    surface, residual, direction = lax.fori_loop(0, ITERS - 1, solve_step, (flat[1], residual, direction))
    surface_out[...] = (surface + direction)[:rows, :cols]

    for step in neighbours:
        moved_copy(step).wait_send()
    for step in sideways:
        for batch in range(2):
            pack_copy(batch, *step).wait_send()

    def drain(group, carry):
        for side in range(2):
            row_copy(group, side).wait_send()
        return carry

    lax.fori_loop(0, groups, drain, 0)


def deliver(fields_in, surface_in, u_out, v_out, t_out, s_out, surface_out, sems):
    outputs = (u_out, v_out, t_out, s_out)
    count = u_out.shape[0]
    lead = fields_in.shape[2] - count
    copies = [
        pltpu.make_async_copy(
            fields_in.at[field, tile, pl.ds(lead, count)],
            outputs[field].at[:, pl.ds(tile * LANE, LANE)],
            sems.at[field, tile],
        )
        for field in range(FIELDS)
        for tile in range(fields_in.shape[1])
    ]
    copies.append(pltpu.make_async_copy(surface_in, surface_out, sems.at[FIELDS, 0]))
    for copy in copies:
        copy.start()
    for copy in copies:
        copy.wait()


def body(by_count, bx_count, u, v, t, s, wind, ssh, depth):
    levels, rows, cols = u.shape
    groups = -(-levels // SUB)
    span = rows + 2 * HALO
    room = span + 4
    tiles = cols // LANE
    width = cols + LANE
    f32 = jnp.float32
    flat_shape = (levels * rows, cols)
    args = [item.reshape(flat_shape) for item in (u, v, t, s)]
    own = jax.ShapeDtypeStruct((FIELDS, tiles, groups * SUB * rows, LANE), f32)
    done, surface = pl.pallas_call(
        functools.partial(kernel, levels, rows * by_count, by_count, bx_count),
        out_shape=[pltpu.VMEM(own.shape, f32), pltpu.VMEM(ssh.shape, f32)],
        in_specs=[pl.BlockSpec(memory_space=pltpu.HBM)] * (FIELDS + 3),
        out_specs=[pl.BlockSpec(memory_space=pltpu.VMEM)] * 2,
        scratch_shapes=[
            pltpu.VMEM((groups + 1, FIELDS, room, SUB, width), f32),
            pltpu.VMEM((rows, cols), jnp.int32),
            pltpu.VMEM((2, groups, SUB, LANE), f32),
            pltpu.VMEM((3, 2, groups, SUB, LANE), f32),
            pltpu.VMEM((FIELDS, room, SUB, width), f32),
            pltpu.VMEM((FIELDS, room, SUB, width), f32),
            pltpu.VMEM((2, room, SUB, width), f32),
            pltpu.VMEM((room, SUB, width), f32),
            pltpu.VMEM((room, SUB, width), f32),
            pltpu.VMEM((room, SUB, width), f32),
            pltpu.VMEM((2, room, SUB, width), f32),
            pltpu.VMEM((room, SUB, LANE), f32),
            pltpu.VMEM((2, rows, SUB, cols), f32),
            pltpu.VMEM((2, rows, cols), f32),
            pltpu.VMEM((2, 2, rows, cols), f32),
            pltpu.VMEM((2, 2, rows, LANE), f32),
            pltpu.VMEM((2, 2, 2, rows, LANE), f32),
            pltpu.VMEM((6, span, width), f32),
            pltpu.SemaphoreType.DMA((tiles, FIELDS + 3)),
            pltpu.SemaphoreType.DMA((2, groups)),
            pltpu.SemaphoreType.DMA((2, groups)),
            pltpu.SemaphoreType.DMA((2, 6)),
            pltpu.SemaphoreType.DMA((2, 6)),
            pltpu.SemaphoreType.DMA((8,)),
            pltpu.SemaphoreType.DMA((8,)),
        ],
        compiler_params=pltpu.CompilerParams(
            collective_id=0, has_side_effects=True, vmem_limit_bytes=61 << 20
        ),
    )(*args, wind.reshape(2 * rows, cols), ssh, depth)
    outs = pl.pallas_call(
        deliver,
        out_shape=[jax.ShapeDtypeStruct(flat_shape, f32)] * FIELDS + [jax.ShapeDtypeStruct(ssh.shape, f32)],
        in_specs=[pl.BlockSpec(memory_space=pltpu.VMEM)] * 2,
        out_specs=[pl.BlockSpec(memory_space=pltpu.HBM)] * (FIELDS + 1),
        scratch_shapes=[pltpu.SemaphoreType.DMA((FIELDS + 1, tiles))],
        compiler_params=pltpu.CompilerParams(vmem_limit_bytes=4 << 20),
    )(done, surface)
    return tuple(item.reshape(u.shape) for item in outs[:FIELDS]) + (outs[FIELDS],)


def solution(mesh):
    whole = P(None, "by", "bx")
    flat = P("by", "bx")
    return jax.shard_map(
        functools.partial(body, mesh.shape["by"], mesh.shape["bx"]),
        mesh=mesh,
        in_specs=(whole,) * 5 + (flat, flat),
        out_specs=(whole,) * 4 + (flat,),
        check_vma=False,
    )
```

```python
import functools
import math

import jax
import jax.numpy as jnp
from jax import lax
from jax.experimental import pallas as pl
from jax.experimental.pallas import tpu as pltpu
from jax.sharding import PartitionSpec as P

ITERS = 4
KAPPA = 0.004
ADVECT = 0.25
PRESS = 0.1
WIND = 0.5
PHI = 0.5
DIVERGE = 2.0
LOWER = 0.2
UPPER = 2.0

MESH = pl.DeviceIdType.MESH
FIELDS = 4
HALO = 4
SUB = 8
LANE = 128
BATCH = 4
FIRST = 5
SECOND = 4


def chebyshev_weights(count):
    middle = 0.5 * (UPPER + LOWER)
    half_span = 0.5 * (UPPER - LOWER)
    ratio_value = middle / half_span
    rho_now = 1.0 / ratio_value
    updates = []
    for _ in range(count - 1):
        rho_next = 1.0 / (2.0 * ratio_value - rho_now)
        updates.append((rho_next * rho_now, 2.0 * rho_next / half_span))
        rho_now = rho_next
    return 1.0 / middle, updates


def east(x):
    return pltpu.roll(x, x.shape[1] - 1, 1)


def west(x):
    return pltpu.roll(x, 1, 1)


def north(x):
    return pltpu.roll(x, x.shape[0] - 1, 0)


def south(x):
    return pltpu.roll(x, 1, 0)


def slot_lane(field, row):
    return (field % 2) * 64 + row * 8 + (field // 2) * 4


def turn(x, shift):
    shift = shift % LANE
    return x if shift == 0 else pltpu.roll(x, shift, 1)


def kernel(
    levels, total_rows, by_count, bx_count,
    u_in, v_in, t_in, s_in, wind_in, ssh_in, depth_in,
    own, surface_out,
    ext, depth_own, pack_send, pack_recv,
    lap, mix, press, depth_c, depth_e, depth_n, stress, cor,
    flow_sum, moved, moved_rows, moved_cols, moved_corners, flat,
    in_sem, row_send, row_recv, pack_ss, pack_rs, moved_ss, moved_rs,
):
    inputs = (u_in, v_in, t_in, s_in)
    rows = SUB
    span = rows + 2 * HALO
    width = ext.shape[-1]
    cols = width - LANE
    tiles = cols // LANE
    groups = -(-levels // SUB)
    block = SUB * rows
    lead = groups * SUB - levels
    assert lead >= 2
    by = lax.axis_index("by")
    bx = lax.axis_index("bx")

    def device(step_y, step_x):
        return (lax.rem(by + step_y + by_count, by_count), lax.rem(bx + step_x + bx_count, bx_count))

    has_north = by < by_count - 1
    has_south = by > 0

    def where_block(y, action):
        if y == 0:
            action()
        else:
            pl.when(has_north if y > 0 else has_south)(action)

    neighbours = [(y, x) for y in (-1, 0, 1) for x in (-1, 0, 1) if (y, x) != (0, 0)]

    def load_copies():
        result = []
        for tile in range(tiles):
            lanes = pl.ds(tile * LANE, LANE)
            for field in range(FIELDS):
                result.append(pltpu.make_async_copy(
                    inputs[field].at[:, lanes], own.at[field, tile, pl.ds(lead * rows, levels * rows)], in_sem.at[tile, field]
                ))
            result.append(pltpu.make_async_copy(
                ssh_in.at[:, lanes], own.at[0, tile, pl.ds(rows, rows)], in_sem.at[tile, FIELDS]
            ))
            result.append(pltpu.make_async_copy(
                wind_in.at[:, lanes], own.at[1, tile, pl.ds(0, 2 * rows)], in_sem.at[tile, FIELDS + 1]
            ))
        result.append(pltpu.make_async_copy(depth_in, depth_own, in_sem.at[0, FIELDS + 2]))
        return result

    for copy in load_copies():
        copy.start()

    barrier = pltpu.get_barrier_semaphore()
    for y in (0, 1, -1):

        def greet(y=y):
            for x in (-1, 0, 1):
                if (y, x) != (0, 0):
                    pl.semaphore_signal(barrier, inc=1, device_id=device(y, x), device_id_type=MESH)

        where_block(y, greet)

    lane = lax.broadcasted_iota(jnp.int32, (SUB, LANE), 1)
    for tile in range(tiles):
        for field in range(2, FIELDS):
            own[field, tile, : lead * rows, :] = jnp.zeros((lead * rows, LANE), jnp.float32)
        if lead > 2:
            for field in range(2):
                own[field, tile, 2 * rows : lead * rows, :] = jnp.zeros(((lead - 2) * rows, LANE), jnp.float32)

    def row_copy(group, side):
        source = HALO + rows - HALO if side == 0 else HALO
        target = 0 if side == 0 else HALO + rows
        return pltpu.make_async_remote_copy(
            src_ref=ext.at[group, :, pl.ds(source, HALO), :, pl.ds(0, cols)],
            dst_ref=ext.at[group, :, pl.ds(target, HALO), :, pl.ds(0, cols)],
            send_sem=row_send.at[side, group],
            recv_sem=row_recv.at[side, group],
            device_id=device(1 - 2 * side, 0),
            device_id_type=MESH,
        )

    def send_all(steps, make):
        for y in (0, 1, -1):

            def act(y=y):
                for step in steps:
                    if step[0] == y:
                        make(step).start()

            where_block(y, act)

    def receive_all(steps, make):
        for y in (0, 1, -1):

            def act(y=y):
                for step in steps:
                    if step[0] == y:
                        make(step).wait_recv()

            where_block(-y, act)

    def sent_all(steps, make):
        for y in (0, 1, -1):

            def act(y=y):
                for step in steps:
                    if step[0] == y:
                        make(step).wait_send()

            where_block(y, act)

    def send_rows(group):
        send_all(lengthways, lambda step: row_copy(group, (1 - step[0]) // 2))

    def receive_rows(group):
        receive_all(lengthways, lambda step: row_copy(group, (1 - step[0]) // 2))

    lengthways = [(1, 0), (-1, 0)]

    batches = ((0, BATCH), (BATCH, groups - BATCH))

    def pack_copy(batch, y, x):
        first, count = batches[batch]
        place = 2 * (y % 3) + (1 - x) // 2
        return pltpu.make_async_remote_copy(
            src_ref=pack_send.at[(1 + x) // 2, pl.ds(first, count)],
            dst_ref=pack_recv.at[y % 3, (1 - x) // 2, pl.ds(first, count)],
            send_sem=pack_ss.at[batch, place],
            recv_sem=pack_rs.at[batch, place],
            device_id=device(y, x),
            device_id_type=MESH,
        )

    sideways = [(y, x) for y in (0, 1, -1) for x in (-1, 1)]

    for copy in load_copies():
        copy.wait()
    for tile in range(tiles):
        own[0, tile, :rows, :] = depth_own[:, tile * LANE : (tile + 1) * LANE].astype(jnp.float32)
    pl.semaphore_wait(barrier, 2 + 3 * has_north.astype(jnp.int32) + 3 * has_south.astype(jnp.int32))

    def stage_step(group):
        west_pack = jnp.zeros((SUB, LANE), jnp.float32)
        east_pack = jnp.zeros((SUB, LANE), jnp.float32)
        for field in range(FIELDS):
            for row in range(rows):
                parts = [
                    own[field, tile, pl.ds(group * block + row, SUB, stride=rows), :]
                    for tile in range(tiles)
                ]
                for tile in range(tiles):
                    ext[group, field, HALO + row, :, tile * LANE : (tile + 1) * LANE] = parts[tile]
                first = slot_lane(field, row)
                here = (lane >= first) & (lane < first + HALO)
                west_pack = jnp.where(here, turn(parts[0], first), west_pack)
                east_pack = jnp.where(here, turn(parts[-1], first + HALO), east_pack)
        pack_send[0, group] = west_pack
        pack_send[1, group] = east_pack

    assert groups % BATCH == 0

    def stage_batch(index, carry):
        for k in range(BATCH):
            stage_step(index * BATCH + k)

        @pl.when(index == 0)
        def _():
            send_rows(0)
            send_all(sideways, lambda step: pack_copy(0, *step))

            def more(group, inner):
                send_rows(group)
                return inner

            lax.fori_loop(1, BATCH, more, 0)

        return carry

    lax.fori_loop(0, groups // BATCH, stage_batch, 0)
    send_all(sideways, lambda step: pack_copy(1, *step))

    def send_step(group, carry):
        send_rows(group)
        return carry

    lax.fori_loop(BATCH, groups, send_step, 0)

    row_index = by * rows - HALO + lax.broadcasted_iota(jnp.int32, (span, LANE), 0)
    turning = 1.2 * jnp.sin(0.9 * math.pi * ((row_index.astype(jnp.float32) + 0.5) / total_rows - 0.5))
    for row in range(span):
        cor[row] = jnp.broadcast_to(turning[row : row + 1, :], (SUB, LANE))

    sub = lax.broadcasted_iota(jnp.int32, (SUB, width), 0)
    level = sub.astype(jnp.float32)
    zeros = jnp.zeros((SUB, width), jnp.float32)

    for row in range(span):
        press[0, row] = zeros
        press[1, row] = zeros
    for axis in range(2):
        for row in range(rows):
            flow_sum[axis, row] = jnp.zeros((SUB, cols), jnp.float32)

    def operator(field, corner):
        north_field = north(field)
        total = field + north_field
        change = north_field - field
        flux_x = corner * (0.5 * (east(total) - total))
        flux_y = corner * (0.5 * (east(change) + change))
        along_x = flux_x + south(flux_x)
        along_y = flux_y + west(flux_y)
        return PHI * field - 0.5 * ((along_x - west(along_x)) + (along_y - south(along_y)))

    def flat_tables():
        for row in range(span):
            index = by * rows + (row - HALO)
            inside = (index >= 0) & (index < total_rows)
            here = jnp.where(inside, jnp.broadcast_to(ext[0, 0, row, 0:1, :], (SUB, width)), 0.0)
            depth_c[row] = here
            depth_e[row] = jnp.minimum(here, east(here))
            if row > 0:
                depth_n[row - 1] = jnp.minimum(before, here)
            before = here
            for axis in range(2):
                wind = jnp.broadcast_to(ext[0, 1, row, axis : axis + 1, :], (SUB, width))
                stress[axis, row] = jnp.where(sub == lead, WIND * wind, 0.0)
            place = (row + span - HALO) % span
            flat[0, place : place + 1, :] = here[0:1, :]
            flat[1, place : place + 1, :] = jnp.where(inside, ext[0, 0, row, 1:2, :], 0.0)
        depth = flat[0]
        ssh = flat[1]
        near = jnp.minimum(depth, east(depth))
        corner = jnp.minimum(near, north(near)) * (1.0 / levels)
        pair = corner + west(corner)
        ocean = jnp.where(depth > 0.0, 1.0, 0.0)
        flat[2] = corner
        flat[3] = 1.0 / (PHI + 0.5 * (pair + south(pair)))
        flat[4] = ocean
        flat[5] = ocean * (PHI * ssh) - operator(ssh, corner)

    def cut(mask, value):
        return jnp.where(mask, value, 0.0)

    def tendencies(group):
        number = level + (group * SUB - lead).astype(jnp.float32)
        number = jnp.where(number < 0.0, 1e9, number)

        def stage_pass(part):
            slot = group if part == 0 else groups
            keep = width if part == 0 else cols

            def first_block(index, inner):
                row = 1 + 2 * part + index * FIRST
                wet = [number < depth_c[row + k] for k in range(FIRST)]
                wet_e = [number < depth_e[row + k] for k in range(FIRST)]
                wet_n = [number < depth_n[row - 1 + k] for k in range(FIRST + 1)]
                speed = [
                    [(-0.5 * ADVECT) * ext[slot, field, row + k] for field in range(2)] for k in range(FIRST)
                ]
                for field in range(FIELDS):
                    cells = [ext[slot, field, row - 1 + k] for k in range(FIRST + 2)]
                    faces = [cut(wet_n[k], cells[k + 1] - cells[k]) for k in range(FIRST + 1)]
                    for k in range(FIRST):
                        here = cells[k + 1]
                        face_e = cut(wet_e[k], east(here) - here)
                        face_w = west(face_e)
                        lap[field, row + k] = (face_e - face_w) + (faces[k + 1] - faces[k])
                        mix[field, row + k] = speed[k][0] * (face_e + face_w) + speed[k][1] * (
                            faces[k + 1] + faces[k]
                        )
                above = [
                    jnp.broadcast_to(press[part, row + k, SUB - 1 : SUB, :], (SUB, width)) for k in range(FIRST)
                ]
                for k in range(FIRST):
                    running = cut(
                        wet[k],
                        (-0.8 * PRESS) * ext[slot, 2, row + k] + (0.6 * PRESS) * ext[slot, 3, row + k],
                    )
                    for shift in (1, 2, 4):
                        running = running + jnp.where(sub >= shift, pltpu.roll(running, shift, 0), 0.0)
                    press[part, row + k] = above[k] + running
                return inner

            def second_block(index, inner):
                row = 2 + 2 * part + index * SECOND
                wet = [(number < depth_c[row + k])[:, :keep] for k in range(SECOND)]
                wet_e = [number < depth_e[row + k] for k in range(SECOND)]
                wet_n = [(number < depth_n[row - 1 + k])[:, :keep] for k in range(SECOND + 1)]

                def differences(cells):
                    faces = [
                        cut(wet_n[k], cells[k + 1][:, :keep] - cells[k][:, :keep]) for k in range(SECOND + 1)
                    ]
                    result = []
                    for k in range(SECOND):
                        here = cells[k + 1]
                        face_e = cut(wet_e[k], east(here) - here)
                        result.append((face_e[:, :keep], west(face_e)[:, :keep], faces[k + 1], faces[k]))
                    return result

                forced = []
                cells = [press[part, row - 1 + k] for k in range(SECOND + 2)]
                for k, (face_e, face_w, face_n, face_s) in enumerate(differences(cells)):
                    turned = jnp.concatenate([cor[row + k]] * (keep // LANE), axis=1)
                    forced.append((
                        cut(wet[k], turned * ext[slot, 1, row + k, :, :keep]) - 0.5 * (face_e + face_w),
                        cut(wet[k], -turned * ext[slot, 0, row + k, :, :keep]) - 0.5 * (face_n + face_s),
                    ))
                results = []
                for field in range(FIELDS):
                    cells = [lap[field, row - 1 + k] for k in range(SECOND + 2)]
                    for k, (face_e, face_w, face_n, face_s) in enumerate(differences(cells)):
                        twice = (face_e - face_w) + (face_n - face_s)
                        value = (
                            ext[slot, field, row + k, :, :keep] + mix[field, row + k, :, :keep]
                        ) - KAPPA * twice
                        if field < 2:
                            value = value + forced[k][field]
                        if part == 1:
                            value = 0.5 * (ext[group, field, row + k, :, :keep] + value)
                        results.append((field, k, value))
                for field, k, value in results:
                    if part == 0:
                        ext[groups, field, row + k] = value
                        continue
                    inner_row = row + k - HALO
                    for tile in range(tiles):
                        own[field, tile, pl.ds(group * block + inner_row, SUB, stride=rows), :] = value[
                            :, tile * LANE : (tile + 1) * LANE
                        ]
                    if field < 2:
                        flow_sum[field, inner_row] = flow_sum[field, inner_row] + cut(wet[k], value)
                return inner

            lax.fori_loop(0, (span - 2 - 4 * part + FIRST - 1) // FIRST, first_block, 0)
            lax.fori_loop(0, (span - 4 - 4 * part + SECOND - 1) // SECOND, second_block, 0)

            @pl.when(group == 0)
            def _():
                for row in range(2 + 2 * part, span - 2 - 2 * part):
                    for axis in range(2):
                        wind = cut(number < depth_c[row], stress[axis, row])
                        if part == 0:
                            ext[groups, axis, row] = ext[groups, axis, row] + wind
                            continue
                        half = 0.5 * wind[:, :cols]
                        flow_sum[axis, row - HALO] = flow_sum[axis, row - HALO] + half
                        for tile in range(tiles):
                            place = pl.ds(row - HALO, SUB, stride=rows)
                            lanes = slice(tile * LANE, (tile + 1) * LANE)
                            own[axis, tile, place, :] = own[axis, tile, place, :] + half[:, lanes]

        stage_pass(0)
        stage_pass(1)

    west_lanes = (lane & 7) < HALO

    def widen(group):
        packs = [[pack_recv[y, x, group] for x in range(2)] for y in range(3)]
        for field in range(FIELDS):
            shifts = (
                HALO * 8 - slot_lane(field, 0), -slot_lane(field, rows - HALO), (HALO + rows) * 8 - slot_lane(field, 0)
            )
            parts = [
                jnp.where(west_lanes, turn(packs[y][0], shifts[y]), turn(packs[y][1], shifts[y] + HALO))
                for y in range(3)
            ]
            all_rows = jnp.where(
                lane < HALO * 8, parts[1], jnp.where(lane < (HALO + rows) * 8, parts[0], parts[2])
            )
            for row in range(span):
                ext[group, field, row, :, cols:width] = turn(all_rows, LANE - HALO - 8 * row)

    receive_all(sideways, lambda step: pack_copy(0, *step))
    receive_rows(0)
    widen(0)
    flat_tables()

    def group_step(group, carry):
        @pl.when(group == BATCH)
        def _():
            receive_all(sideways, lambda step: pack_copy(1, *step))

        @pl.when(group > 0)
        def _():
            receive_rows(group)
            widen(group)

        tendencies(group)
        return carry

    lax.fori_loop(0, groups, group_step, 0)

    for row in range(rows):
        for axis in range(2):
            total = jnp.sum(flow_sum[axis, row], axis=0, keepdims=True) * (1.0 / levels)
            moved[axis, row : row + 1, :] = total

    def moved_copy(step):
        y, x = step
        place = neighbours.index(step)
        other = neighbours.index((-y, -x))
        if x == 0:
            source, target = moved, moved_rows.at[(1 - y) // 2]
        else:
            tile = tiles - 1 if x > 0 else 0
            source = moved.at[:, :, pl.ds(tile * LANE, LANE)]
            side = (1 - x) // 2
            target = moved_cols.at[side] if y == 0 else moved_corners.at[(1 - y) // 2, side]
        return pltpu.make_async_remote_copy(
            src_ref=source, dst_ref=target, send_sem=moved_ss.at[place], recv_sem=moved_rs.at[place],
            device_id=device(y, x), device_id_type=MESH,
        )

    send_all(neighbours, moved_copy)
    receive_all(neighbours, moved_copy)
    lower = lax.broadcasted_iota(jnp.int32, (SUB, cols), 0) < HALO
    lower_tile = lax.broadcasted_iota(jnp.int32, (SUB, LANE), 0) < HALO
    right = lane < LANE // 2
    def given(side, values):
        return jnp.where(has_north if side == 1 else has_south, values, 0.0)

    transports = []
    for axis in range(2):
        near = jnp.concatenate(
            [moved[axis], jnp.where(right, moved_cols[1, axis], moved_cols[0, axis])], axis=1
        )
        corners = [
            jnp.where(right, moved_corners[side, 1, axis], moved_corners[side, 0, axis]) for side in range(2)
        ]
        far = jnp.concatenate(
            [
                jnp.where(lower, given(1, moved_rows[1, axis]), given(0, moved_rows[0, axis])),
                jnp.where(lower_tile, given(1, corners[1]), given(0, corners[0])),
            ],
            axis=1,
        )
        transports.append(jnp.concatenate([near, far], axis=0))

    corner = flat[2]
    diagonal_inverse = flat[3]
    ocean = flat[4]
    face_x = ocean * east(ocean) * (east(transports[0]) - transports[0])
    face_y = ocean * north(ocean) * (north(transports[1]) - transports[1])
    spread = 0.5 * ((face_x + west(face_x)) + (face_y + south(face_y)))
    residual = flat[5] - (DIVERGE * ocean) * spread
    opening, updates = chebyshev_weights(ITERS)
    direction = opening * (residual * diagonal_inverse)

    def pick(index, values):
        result = jnp.float32(values[-1])
        for k in range(len(values) - 1):
            result = jnp.where(index == k, jnp.float32(values[k]), result)
        return result

    def solve_step(index, carry):
        surface, residual, direction = carry
        surface = surface + direction
        residual = residual - operator(direction, corner)
        keep = pick(index, [item[0] for item in updates])
        push = pick(index, [item[1] for item in updates])
        direction = keep * direction + push * (residual * diagonal_inverse)
        return surface, residual, direction

    surface, residual, direction = lax.fori_loop(0, ITERS - 1, solve_step, (flat[1], residual, direction))
    surface_out[...] = (surface + direction)[:rows, :cols]

    sent_all(neighbours, moved_copy)
    for batch in range(2):
        sent_all(sideways, lambda step: pack_copy(batch, *step))

    def drain(group, carry):
        sent_all(lengthways, lambda step: row_copy(group, (1 - step[0]) // 2))
        return carry

    lax.fori_loop(0, groups, drain, 0)


def deliver(lead, fields_in, surface_in, u_out, v_out, t_out, s_out, surface_out, sems):
    outputs = (u_out, v_out, t_out, s_out)
    count = u_out.shape[0]
    copies = [
        pltpu.make_async_copy(
            fields_in.at[field, tile, pl.ds(lead, count)],
            outputs[field].at[:, pl.ds(tile * LANE, LANE)],
            sems.at[field, tile],
        )
        for field in range(FIELDS)
        for tile in range(fields_in.shape[1])
    ]
    copies.append(pltpu.make_async_copy(surface_in, surface_out, sems.at[FIELDS, 0]))
    for copy in copies:
        copy.start()
    for copy in copies:
        copy.wait()


def body(by_count, bx_count, u, v, t, s, wind, ssh, depth):
    levels, rows, cols = u.shape
    groups = -(-levels // SUB)
    span = rows + 2 * HALO
    room = span + 4
    tiles = cols // LANE
    width = cols + LANE
    f32 = jnp.float32
    flat_shape = (levels * rows, cols)
    args = [item.reshape(flat_shape) for item in (u, v, t, s)]
    own = jax.ShapeDtypeStruct((FIELDS, tiles, (groups + 1) * SUB * rows, LANE), f32)
    done, surface = pl.pallas_call(
        functools.partial(kernel, levels, rows * by_count, by_count, bx_count),
        out_shape=[pltpu.VMEM(own.shape, f32), pltpu.VMEM(ssh.shape, f32)],
        in_specs=[pl.BlockSpec(memory_space=pltpu.HBM)] * (FIELDS + 3),
        out_specs=[pl.BlockSpec(memory_space=pltpu.VMEM)] * 2,
        scratch_shapes=[
            pltpu.VMEM((groups + 1, FIELDS, room, SUB, width), f32),
            pltpu.VMEM((rows, cols), jnp.int32),
            pltpu.VMEM((2, groups, SUB, LANE), f32),
            pltpu.VMEM((3, 2, groups, SUB, LANE), f32),
            pltpu.VMEM((FIELDS, room, SUB, width), f32),
            pltpu.VMEM((FIELDS, room, SUB, width), f32),
            pltpu.VMEM((2, room, SUB, width), f32),
            pltpu.VMEM((room, SUB, width), f32),
            pltpu.VMEM((room, SUB, width), f32),
            pltpu.VMEM((room, SUB, width), f32),
            pltpu.VMEM((2, room, SUB, width), f32),
            pltpu.VMEM((room, SUB, LANE), f32),
            pltpu.VMEM((2, rows, SUB, cols), f32),
            pltpu.VMEM((2, rows, cols), f32),
            pltpu.VMEM((2, 2, rows, cols), f32),
            pltpu.VMEM((2, 2, rows, LANE), f32),
            pltpu.VMEM((2, 2, 2, rows, LANE), f32),
            pltpu.VMEM((6, span, width), f32),
            pltpu.SemaphoreType.DMA((tiles, FIELDS + 3)),
            pltpu.SemaphoreType.DMA((2, groups)),
            pltpu.SemaphoreType.DMA((2, groups)),
            pltpu.SemaphoreType.DMA((2, 6)),
            pltpu.SemaphoreType.DMA((2, 6)),
            pltpu.SemaphoreType.DMA((8,)),
            pltpu.SemaphoreType.DMA((8,)),
        ],
        compiler_params=pltpu.CompilerParams(
            collective_id=0, has_side_effects=True, vmem_limit_bytes=61 << 20
        ),
    )(*args, wind.reshape(2 * rows, cols), ssh, depth)
    outs = pl.pallas_call(
        functools.partial(deliver, (groups * SUB - levels) * rows),
        out_shape=[jax.ShapeDtypeStruct(flat_shape, f32)] * FIELDS + [jax.ShapeDtypeStruct(ssh.shape, f32)],
        in_specs=[pl.BlockSpec(memory_space=pltpu.VMEM)] * 2,
        out_specs=[pl.BlockSpec(memory_space=pltpu.HBM)] * (FIELDS + 1),
        scratch_shapes=[pltpu.SemaphoreType.DMA((FIELDS + 1, tiles))],
        compiler_params=pltpu.CompilerParams(vmem_limit_bytes=4 << 20),
    )(done, surface)
    return tuple(item.reshape(u.shape) for item in outs[:FIELDS]) + (outs[FIELDS],)


def solution(mesh):
    whole = P(None, "by", "bx")
    flat = P("by", "bx")
    return jax.shard_map(
        functools.partial(body, mesh.shape["by"], mesh.shape["bx"]),
        mesh=mesh,
        in_specs=(whole,) * 5 + (flat, flat),
        out_specs=(whole,) * 4 + (flat,),
        check_vma=False,
    )
```

```python
import functools
import math

import jax
import jax.numpy as jnp
from jax import lax
from jax.experimental import pallas as pl
from jax.experimental.pallas import tpu as pltpu
from jax.sharding import PartitionSpec as P

ITERS = 4
KAPPA = 0.004
ADVECT = 0.25
PRESS = 0.1
WIND = 0.5
PHI = 0.5
DIVERGE = 2.0
LOWER = 0.2
UPPER = 2.0

MESH = pl.DeviceIdType.MESH
FIELDS = 4
HALO = 4
SUB = 8
LANE = 128
BATCH = 4
FIRST = 5
SECOND = 4


def chebyshev_weights(count):
    middle = 0.5 * (UPPER + LOWER)
    half_span = 0.5 * (UPPER - LOWER)
    ratio_value = middle / half_span
    rho_now = 1.0 / ratio_value
    updates = []
    for _ in range(count - 1):
        rho_next = 1.0 / (2.0 * ratio_value - rho_now)
        updates.append((rho_next * rho_now, 2.0 * rho_next / half_span))
        rho_now = rho_next
    return 1.0 / middle, updates


def east(x):
    return pltpu.roll(x, x.shape[1] - 1, 1)


def west(x):
    return pltpu.roll(x, 1, 1)


def north(x):
    return pltpu.roll(x, x.shape[0] - 1, 0)


def south(x):
    return pltpu.roll(x, 1, 0)


def slot_lane(field, row):
    return (field % 2) * 64 + row * 8 + (field // 2) * 4


def turn(x, shift):
    shift = shift % LANE
    return x if shift == 0 else pltpu.roll(x, shift, 1)


def kernel(
    levels, total_rows, by_count, bx_count,
    u_in, v_in, t_in, s_in, wind_in, ssh_in, depth_in,
    own, surface_out,
    ext, depth_own, pack_send, pack_recv, far_send, far_recv,
    lap, mix, press, depth_c, depth_e, depth_n, stress, cor,
    flow_sum, moved, moved_rows, moved_cols, moved_corners, flat,
    in_sem, row_send, row_recv, pack_ss, pack_rs, moved_ss, moved_rs,
):
    inputs = (u_in, v_in, t_in, s_in)
    rows = SUB
    span = rows + 2 * HALO
    width = ext.shape[-1]
    cols = width - LANE
    tiles = cols // LANE
    groups = -(-levels // SUB)
    block = SUB * rows
    lead = groups * SUB - levels
    assert lead >= 2
    by = lax.axis_index("by")
    bx = lax.axis_index("bx")

    def device(step_y, step_x):
        return (lax.rem(by + step_y + by_count, by_count), lax.rem(bx + step_x + bx_count, bx_count))

    has_north = by < by_count - 1
    has_south = by > 0

    def where_block(y, action):
        if y == 0:
            action()
        else:
            pl.when(has_north if y > 0 else has_south)(action)

    neighbours = [(y, x) for y in (-1, 0, 1) for x in (-1, 0, 1) if (y, x) != (0, 0)]

    def load_copies():
        result = []
        for tile in range(tiles):
            lanes = pl.ds(tile * LANE, LANE)
            for field in range(FIELDS):
                result.append(pltpu.make_async_copy(
                    inputs[field].at[:, lanes], own.at[field, tile, pl.ds(lead * rows, levels * rows)], in_sem.at[tile, field]
                ))
            result.append(pltpu.make_async_copy(
                ssh_in.at[:, lanes], own.at[0, tile, pl.ds(rows, rows)], in_sem.at[tile, FIELDS]
            ))
            result.append(pltpu.make_async_copy(
                wind_in.at[:, lanes], own.at[1, tile, pl.ds(0, 2 * rows)], in_sem.at[tile, FIELDS + 1]
            ))
        result.append(pltpu.make_async_copy(depth_in, depth_own, in_sem.at[0, FIELDS + 2]))
        return result

    for copy in load_copies():
        copy.start()

    barrier = pltpu.get_barrier_semaphore()
    for y in (0, 1, -1):

        def greet(y=y):
            for x in (-1, 0, 1):
                if (y, x) != (0, 0):
                    pl.semaphore_signal(barrier, inc=1, device_id=device(y, x), device_id_type=MESH)

        where_block(y, greet)

    lane = lax.broadcasted_iota(jnp.int32, (SUB, LANE), 1)
    for tile in range(tiles):
        for field in range(2, FIELDS):
            own[field, tile, : lead * rows, :] = jnp.zeros((lead * rows, LANE), jnp.float32)
        if lead > 2:
            for field in range(2):
                own[field, tile, 2 * rows : lead * rows, :] = jnp.zeros(((lead - 2) * rows, LANE), jnp.float32)

    def row_copy(group, side):
        source = HALO + rows - HALO if side == 0 else HALO
        target = 0 if side == 0 else HALO + rows
        return pltpu.make_async_remote_copy(
            src_ref=ext.at[group, :, pl.ds(source, HALO), :, pl.ds(0, cols)],
            dst_ref=ext.at[group, :, pl.ds(target, HALO), :, pl.ds(0, cols)],
            send_sem=row_send.at[side, group],
            recv_sem=row_recv.at[side, group],
            device_id=device(1 - 2 * side, 0),
            device_id_type=MESH,
        )

    def send_all(steps, make):
        for y in (0, 1, -1):

            def act(y=y):
                for step in steps:
                    if step[0] == y:
                        make(step).start()

            where_block(y, act)

    def receive_all(steps, make):
        for y in (0, 1, -1):

            def act(y=y):
                for step in steps:
                    if step[0] == y:
                        make(step).wait_recv()

            where_block(-y, act)

    def sent_all(steps, make):
        for y in (0, 1, -1):

            def act(y=y):
                for step in steps:
                    if step[0] == y:
                        make(step).wait_send()

            where_block(y, act)

    def send_rows(group):
        send_all(lengthways, lambda step: row_copy(group, (1 - step[0]) // 2))

    def receive_rows(group):
        receive_all(lengthways, lambda step: row_copy(group, (1 - step[0]) // 2))

    lengthways = [(1, 0), (-1, 0)]

    batches = ((0, BATCH), (BATCH, groups - BATCH))

    def pack_copy(batch, y, x):
        first, count = batches[batch]
        place = 2 * (y % 3) + (1 - x) // 2
        if y == 0:
            source = pack_send.at[(1 + x) // 2, pl.ds(first, count)]
            target = pack_recv.at[(1 - x) // 2, pl.ds(first, count)]
        else:
            source = far_send.at[(1 - y) // 2, (1 + x) // 2, pl.ds(first // 2, count // 2)]
            target = far_recv.at[(1 - y) // 2, (1 - x) // 2, pl.ds(first // 2, count // 2)]
        return pltpu.make_async_remote_copy(
            src_ref=source,
            dst_ref=target,
            send_sem=pack_ss.at[batch, place],
            recv_sem=pack_rs.at[batch, place],
            device_id=device(y, x),
            device_id_type=MESH,
        )

    sideways = [(y, x) for y in (0, 1, -1) for x in (-1, 1)]

    for copy in load_copies():
        copy.wait()
    for tile in range(tiles):
        own[0, tile, :rows, :] = depth_own[:, tile * LANE : (tile + 1) * LANE].astype(jnp.float32)
    pl.semaphore_wait(barrier, 2 + 3 * has_north.astype(jnp.int32) + 3 * has_south.astype(jnp.int32))

    def stage_step(group):
        west_pack = jnp.zeros((SUB, LANE), jnp.float32)
        east_pack = jnp.zeros((SUB, LANE), jnp.float32)
        for field in range(FIELDS):
            for row in range(rows):
                parts = [
                    own[field, tile, pl.ds(group * block + row, SUB, stride=rows), :]
                    for tile in range(tiles)
                ]
                for tile in range(tiles):
                    ext[group, field, HALO + row, :, tile * LANE : (tile + 1) * LANE] = parts[tile]
                first = slot_lane(field, row)
                here = (lane >= first) & (lane < first + HALO)
                west_pack = jnp.where(here, turn(parts[0], first), west_pack)
                east_pack = jnp.where(here, turn(parts[-1], first + HALO), east_pack)
        pack_send[0, group] = west_pack
        pack_send[1, group] = east_pack
        return west_pack, east_pack

    assert groups % BATCH == 0 and BATCH % 2 == 0
    upper = (lane & 32) != 0

    def stage_batch(index, carry):
        for k in range(BATCH // 2):
            pair = index * (BATCH // 2) + k
            packs = stage_step(2 * pair), stage_step(2 * pair + 1)
            for side in range(2):
                far_send[0, side, pair] = jnp.where(upper, packs[0][side], turn(packs[1][side], -32))
                far_send[1, side, pair] = jnp.where(upper, turn(packs[1][side], 32), packs[0][side])

        @pl.when(index == 0)
        def _():
            send_rows(0)
            send_all(sideways, lambda step: pack_copy(0, *step))

            def more(group, inner):
                send_rows(group)
                return inner

            lax.fori_loop(1, BATCH, more, 0)

        return carry

    lax.fori_loop(0, groups // BATCH, stage_batch, 0)
    send_all(sideways, lambda step: pack_copy(1, *step))

    def send_step(group, carry):
        send_rows(group)
        return carry

    lax.fori_loop(BATCH, groups, send_step, 0)

    row_index = by * rows - HALO + lax.broadcasted_iota(jnp.int32, (span, LANE), 0)
    turning = 1.2 * jnp.sin(0.9 * math.pi * ((row_index.astype(jnp.float32) + 0.5) / total_rows - 0.5))
    for row in range(span):
        cor[row] = jnp.broadcast_to(turning[row : row + 1, :], (SUB, LANE))

    sub = lax.broadcasted_iota(jnp.int32, (SUB, width), 0)
    level = sub.astype(jnp.float32)
    zeros = jnp.zeros((SUB, width), jnp.float32)

    for row in range(span):
        press[0, row] = zeros
        press[1, row] = zeros
    for axis in range(2):
        for row in range(rows):
            flow_sum[axis, row] = jnp.zeros((SUB, cols), jnp.float32)

    def operator(field, corner):
        north_field = north(field)
        total = field + north_field
        change = north_field - field
        flux_x = corner * (0.5 * (east(total) - total))
        flux_y = corner * (0.5 * (east(change) + change))
        along_x = flux_x + south(flux_x)
        along_y = flux_y + west(flux_y)
        return PHI * field - 0.5 * ((along_x - west(along_x)) + (along_y - south(along_y)))

    def flat_tables():
        for row in range(span):
            index = by * rows + (row - HALO)
            inside = (index >= 0) & (index < total_rows)
            here = jnp.where(inside, jnp.broadcast_to(ext[0, 0, row, 0:1, :], (SUB, width)), 0.0)
            depth_c[row] = here
            depth_e[row] = jnp.minimum(here, east(here))
            if row > 0:
                depth_n[row - 1] = jnp.minimum(before, here)
            before = here
            for axis in range(2):
                wind = jnp.broadcast_to(ext[0, 1, row, axis : axis + 1, :], (SUB, width))
                stress[axis, row] = jnp.where(sub == lead, WIND * wind, 0.0)
            place = (row + span - HALO) % span
            flat[0, place : place + 1, :] = here[0:1, :]
            flat[1, place : place + 1, :] = jnp.where(inside, ext[0, 0, row, 1:2, :], 0.0)
        depth = flat[0]
        ssh = flat[1]
        near = jnp.minimum(depth, east(depth))
        corner = jnp.minimum(near, north(near)) * (1.0 / levels)
        pair = corner + west(corner)
        ocean = jnp.where(depth > 0.0, 1.0, 0.0)
        flat[2] = corner
        flat[3] = 1.0 / (PHI + 0.5 * (pair + south(pair)))
        flat[4] = ocean
        flat[5] = ocean * (PHI * ssh) - operator(ssh, corner)

    def cut(mask, value):
        return jnp.where(mask, value, 0.0)

    def tendencies(group):
        number = level + (group * SUB - lead).astype(jnp.float32)
        number = jnp.where(number < 0.0, 1e9, number)

        def stage_pass(part):
            slot = group if part == 0 else groups
            keep = width if part == 0 else cols

            def first_block(index, inner):
                row = 1 + 2 * part + index * FIRST
                wet = [number < depth_c[row + k] for k in range(FIRST)]
                wet_e = [number < depth_e[row + k] for k in range(FIRST)]
                wet_n = [number < depth_n[row - 1 + k] for k in range(FIRST + 1)]
                speed = [
                    [(-0.5 * ADVECT) * ext[slot, field, row + k] for field in range(2)] for k in range(FIRST)
                ]
                for field in range(FIELDS):
                    cells = [ext[slot, field, row - 1 + k] for k in range(FIRST + 2)]
                    faces = [cut(wet_n[k], cells[k + 1] - cells[k]) for k in range(FIRST + 1)]
                    for k in range(FIRST):
                        here = cells[k + 1]
                        face_e = cut(wet_e[k], east(here) - here)
                        face_w = west(face_e)
                        lap[field, row + k] = (face_e - face_w) + (faces[k + 1] - faces[k])
                        mix[field, row + k] = speed[k][0] * (face_e + face_w) + speed[k][1] * (
                            faces[k + 1] + faces[k]
                        )
                above = [
                    jnp.broadcast_to(press[part, row + k, SUB - 1 : SUB, :], (SUB, width)) for k in range(FIRST)
                ]
                for k in range(FIRST):
                    running = cut(
                        wet[k],
                        (-0.8 * PRESS) * ext[slot, 2, row + k] + (0.6 * PRESS) * ext[slot, 3, row + k],
                    )
                    for shift in (1, 2, 4):
                        running = running + jnp.where(sub >= shift, pltpu.roll(running, shift, 0), 0.0)
                    press[part, row + k] = above[k] + running
                return inner

            def second_block(index, inner):
                row = 2 + 2 * part + index * SECOND
                wet = [(number < depth_c[row + k])[:, :keep] for k in range(SECOND)]
                wet_e = [number < depth_e[row + k] for k in range(SECOND)]
                wet_n = [(number < depth_n[row - 1 + k])[:, :keep] for k in range(SECOND + 1)]

                def differences(cells):
                    faces = [
                        cut(wet_n[k], cells[k + 1][:, :keep] - cells[k][:, :keep]) for k in range(SECOND + 1)
                    ]
                    result = []
                    for k in range(SECOND):
                        here = cells[k + 1]
                        face_e = cut(wet_e[k], east(here) - here)
                        result.append((face_e[:, :keep], west(face_e)[:, :keep], faces[k + 1], faces[k]))
                    return result

                forced = []
                cells = [press[part, row - 1 + k] for k in range(SECOND + 2)]
                for k, (face_e, face_w, face_n, face_s) in enumerate(differences(cells)):
                    turned = jnp.concatenate([cor[row + k]] * (keep // LANE), axis=1)
                    forced.append((
                        cut(wet[k], turned * ext[slot, 1, row + k, :, :keep]) - 0.5 * (face_e + face_w),
                        cut(wet[k], -turned * ext[slot, 0, row + k, :, :keep]) - 0.5 * (face_n + face_s),
                    ))
                results = []
                for field in range(FIELDS):
                    cells = [lap[field, row - 1 + k] for k in range(SECOND + 2)]
                    for k, (face_e, face_w, face_n, face_s) in enumerate(differences(cells)):
                        twice = (face_e - face_w) + (face_n - face_s)
                        value = (
                            ext[slot, field, row + k, :, :keep] + mix[field, row + k, :, :keep]
                        ) - KAPPA * twice
                        if field < 2:
                            value = value + forced[k][field]
                        if part == 1:
                            value = 0.5 * (ext[group, field, row + k, :, :keep] + value)
                        results.append((field, k, value))
                for field, k, value in results:
                    if part == 0:
                        ext[groups, field, row + k] = value
                        continue
                    inner_row = row + k - HALO
                    for tile in range(tiles):
                        own[field, tile, pl.ds(group * block + inner_row, SUB, stride=rows), :] = value[
                            :, tile * LANE : (tile + 1) * LANE
                        ]
                    if field < 2:
                        flow_sum[field, inner_row] = flow_sum[field, inner_row] + cut(wet[k], value)
                return inner

            lax.fori_loop(0, (span - 2 - 4 * part + FIRST - 1) // FIRST, first_block, 0)
            lax.fori_loop(0, (span - 4 - 4 * part + SECOND - 1) // SECOND, second_block, 0)

            @pl.when(group == 0)
            def _():
                for row in range(2 + 2 * part, span - 2 - 2 * part):
                    for axis in range(2):
                        wind = cut(number < depth_c[row], stress[axis, row])
                        if part == 0:
                            ext[groups, axis, row] = ext[groups, axis, row] + wind
                            continue
                        half = 0.5 * wind[:, :cols]
                        flow_sum[axis, row - HALO] = flow_sum[axis, row - HALO] + half
                        for tile in range(tiles):
                            place = pl.ds(row - HALO, SUB, stride=rows)
                            lanes = slice(tile * LANE, (tile + 1) * LANE)
                            own[axis, tile, place, :] = own[axis, tile, place, :] + half[:, lanes]

        stage_pass(0)
        stage_pass(1)

    west_lanes = (lane & 7) < HALO

    def widen(group):
        pair = lax.div(jnp.int32(group), jnp.int32(2))
        odd = lax.rem(jnp.int32(group), jnp.int32(2))
        packs = [
            [pack_recv[x, group] for x in range(2)],
            [pltpu.roll(far_recv[0, x, pair], 32 * odd, 1) for x in range(2)],
            [pltpu.roll(far_recv[1, x, pair], 96 * odd, 1) for x in range(2)],
        ]
        for field in range(FIELDS):
            shifts = (
                HALO * 8 - slot_lane(field, 0), -slot_lane(field, rows - HALO), (HALO + rows) * 8 - slot_lane(field, 0)
            )
            parts = [
                jnp.where(west_lanes, turn(packs[y][0], shifts[y]), turn(packs[y][1], shifts[y] + HALO))
                for y in range(3)
            ]
            all_rows = jnp.where(
                lane < HALO * 8, parts[1], jnp.where(lane < (HALO + rows) * 8, parts[0], parts[2])
            )
            for row in range(span):
                ext[group, field, row, :, cols:width] = turn(all_rows, LANE - HALO - 8 * row)

    receive_all(sideways, lambda step: pack_copy(0, *step))
    receive_rows(0)
    widen(0)
    flat_tables()

    def group_step(group, carry):
        @pl.when(group == BATCH)
        def _():
            receive_all(sideways, lambda step: pack_copy(1, *step))

        @pl.when(group > 0)
        def _():
            receive_rows(group)
            widen(group)

        tendencies(group)
        return carry

    lax.fori_loop(0, groups, group_step, 0)

    for row in range(rows):
        for axis in range(2):
            total = jnp.sum(flow_sum[axis, row], axis=0, keepdims=True) * (1.0 / levels)
            moved[axis, row : row + 1, :] = total

    def moved_copy(step):
        y, x = step
        place = neighbours.index(step)
        other = neighbours.index((-y, -x))
        if x == 0:
            source, target = moved, moved_rows.at[(1 - y) // 2]
        else:
            tile = tiles - 1 if x > 0 else 0
            source = moved.at[:, :, pl.ds(tile * LANE, LANE)]
            side = (1 - x) // 2
            target = moved_cols.at[side] if y == 0 else moved_corners.at[(1 - y) // 2, side]
        return pltpu.make_async_remote_copy(
            src_ref=source, dst_ref=target, send_sem=moved_ss.at[place], recv_sem=moved_rs.at[place],
            device_id=device(y, x), device_id_type=MESH,
        )

    send_all(neighbours, moved_copy)
    receive_all(neighbours, moved_copy)
    lower = lax.broadcasted_iota(jnp.int32, (SUB, cols), 0) < HALO
    lower_tile = lax.broadcasted_iota(jnp.int32, (SUB, LANE), 0) < HALO
    right = lane < LANE // 2
    def given(side, values):
        return jnp.where(has_north if side == 1 else has_south, values, 0.0)

    transports = []
    for axis in range(2):
        near = jnp.concatenate(
            [moved[axis], jnp.where(right, moved_cols[1, axis], moved_cols[0, axis])], axis=1
        )
        corners = [
            jnp.where(right, moved_corners[side, 1, axis], moved_corners[side, 0, axis]) for side in range(2)
        ]
        far = jnp.concatenate(
            [
                jnp.where(lower, given(1, moved_rows[1, axis]), given(0, moved_rows[0, axis])),
                jnp.where(lower_tile, given(1, corners[1]), given(0, corners[0])),
            ],
            axis=1,
        )
        transports.append(jnp.concatenate([near, far], axis=0))

    corner = flat[2]
    diagonal_inverse = flat[3]
    ocean = flat[4]
    face_x = ocean * east(ocean) * (east(transports[0]) - transports[0])
    face_y = ocean * north(ocean) * (north(transports[1]) - transports[1])
    spread = 0.5 * ((face_x + west(face_x)) + (face_y + south(face_y)))
    residual = flat[5] - (DIVERGE * ocean) * spread
    opening, updates = chebyshev_weights(ITERS)
    direction = opening * (residual * diagonal_inverse)

    def pick(index, values):
        result = jnp.float32(values[-1])
        for k in range(len(values) - 1):
            result = jnp.where(index == k, jnp.float32(values[k]), result)
        return result

    def solve_step(index, carry):
        surface, residual, direction = carry
        surface = surface + direction
        residual = residual - operator(direction, corner)
        keep = pick(index, [item[0] for item in updates])
        push = pick(index, [item[1] for item in updates])
        direction = keep * direction + push * (residual * diagonal_inverse)
        return surface, residual, direction

    surface, residual, direction = lax.fori_loop(0, ITERS - 1, solve_step, (flat[1], residual, direction))
    surface_out[...] = (surface + direction)[:rows, :cols]

    sent_all(neighbours, moved_copy)
    for batch in range(2):
        sent_all(sideways, lambda step: pack_copy(batch, *step))

    def drain(group, carry):
        sent_all(lengthways, lambda step: row_copy(group, (1 - step[0]) // 2))
        return carry

    lax.fori_loop(0, groups, drain, 0)


def deliver(lead, fields_in, surface_in, u_out, v_out, t_out, s_out, surface_out, sems):
    outputs = (u_out, v_out, t_out, s_out)
    count = u_out.shape[0]
    copies = [
        pltpu.make_async_copy(
            fields_in.at[field, tile, pl.ds(lead, count)],
            outputs[field].at[:, pl.ds(tile * LANE, LANE)],
            sems.at[field, tile],
        )
        for field in range(FIELDS)
        for tile in range(fields_in.shape[1])
    ]
    copies.append(pltpu.make_async_copy(surface_in, surface_out, sems.at[FIELDS, 0]))
    for copy in copies:
        copy.start()
    for copy in copies:
        copy.wait()


def body(by_count, bx_count, u, v, t, s, wind, ssh, depth):
    levels, rows, cols = u.shape
    groups = -(-levels // SUB)
    span = rows + 2 * HALO
    room = span + 4
    tiles = cols // LANE
    width = cols + LANE
    f32 = jnp.float32
    flat_shape = (levels * rows, cols)
    args = [item.reshape(flat_shape) for item in (u, v, t, s)]
    own = jax.ShapeDtypeStruct((FIELDS, tiles, (groups + 1) * SUB * rows, LANE), f32)
    done, surface = pl.pallas_call(
        functools.partial(kernel, levels, rows * by_count, by_count, bx_count),
        out_shape=[pltpu.VMEM(own.shape, f32), pltpu.VMEM(ssh.shape, f32)],
        in_specs=[pl.BlockSpec(memory_space=pltpu.HBM)] * (FIELDS + 3),
        out_specs=[pl.BlockSpec(memory_space=pltpu.VMEM)] * 2,
        scratch_shapes=[
            pltpu.VMEM((groups + 1, FIELDS, room, SUB, width), f32),
            pltpu.VMEM((rows, cols), jnp.int32),
            pltpu.VMEM((2, groups, SUB, LANE), f32),
            pltpu.VMEM((2, groups, SUB, LANE), f32),
            pltpu.VMEM((2, 2, groups // 2, SUB, LANE), f32),
            pltpu.VMEM((2, 2, groups // 2, SUB, LANE), f32),
            pltpu.VMEM((FIELDS, room, SUB, width), f32),
            pltpu.VMEM((FIELDS, room, SUB, width), f32),
            pltpu.VMEM((2, room, SUB, width), f32),
            pltpu.VMEM((room, SUB, width), f32),
            pltpu.VMEM((room, SUB, width), f32),
            pltpu.VMEM((room, SUB, width), f32),
            pltpu.VMEM((2, room, SUB, width), f32),
            pltpu.VMEM((room, SUB, LANE), f32),
            pltpu.VMEM((2, rows, SUB, cols), f32),
            pltpu.VMEM((2, rows, cols), f32),
            pltpu.VMEM((2, 2, rows, cols), f32),
            pltpu.VMEM((2, 2, rows, LANE), f32),
            pltpu.VMEM((2, 2, 2, rows, LANE), f32),
            pltpu.VMEM((6, span, width), f32),
            pltpu.SemaphoreType.DMA((tiles, FIELDS + 3)),
            pltpu.SemaphoreType.DMA((2, groups)),
            pltpu.SemaphoreType.DMA((2, groups)),
            pltpu.SemaphoreType.DMA((2, 6)),
            pltpu.SemaphoreType.DMA((2, 6)),
            pltpu.SemaphoreType.DMA((8,)),
            pltpu.SemaphoreType.DMA((8,)),
        ],
        compiler_params=pltpu.CompilerParams(
            collective_id=0, has_side_effects=True, vmem_limit_bytes=61 << 20
        ),
    )(*args, wind.reshape(2 * rows, cols), ssh, depth)
    outs = pl.pallas_call(
        functools.partial(deliver, (groups * SUB - levels) * rows),
        out_shape=[jax.ShapeDtypeStruct(flat_shape, f32)] * FIELDS + [jax.ShapeDtypeStruct(ssh.shape, f32)],
        in_specs=[pl.BlockSpec(memory_space=pltpu.VMEM)] * 2,
        out_specs=[pl.BlockSpec(memory_space=pltpu.HBM)] * (FIELDS + 1),
        scratch_shapes=[pltpu.SemaphoreType.DMA((FIELDS + 1, tiles))],
        compiler_params=pltpu.CompilerParams(vmem_limit_bytes=4 << 20),
    )(done, surface)
    return tuple(item.reshape(u.shape) for item in outs[:FIELDS]) + (outs[FIELDS],)


def solution(mesh):
    whole = P(None, "by", "bx")
    flat = P("by", "bx")
    return jax.shard_map(
        functools.partial(body, mesh.shape["by"], mesh.shape["bx"]),
        mesh=mesh,
        in_specs=(whole,) * 5 + (flat, flat),
        out_specs=(whole,) * 4 + (flat,),
        check_vma=False,
    )
```

```python
import functools
import math

import jax
import jax.numpy as jnp
from jax import lax
from jax.experimental import pallas as pl
from jax.experimental.pallas import tpu as pltpu
from jax.sharding import PartitionSpec as P

ITERS = 4
KAPPA = 0.004
ADVECT = 0.25
PRESS = 0.1
WIND = 0.5
PHI = 0.5
DIVERGE = 2.0
LOWER = 0.2
UPPER = 2.0

MESH = pl.DeviceIdType.MESH
FIELDS = 4
HALO = 4
SUB = 8
LANE = 128
BATCH = 2
FIRST = 5
SECOND = 4


def chebyshev_weights(count):
    middle = 0.5 * (UPPER + LOWER)
    half_span = 0.5 * (UPPER - LOWER)
    ratio_value = middle / half_span
    rho_now = 1.0 / ratio_value
    updates = []
    for _ in range(count - 1):
        rho_next = 1.0 / (2.0 * ratio_value - rho_now)
        updates.append((rho_next * rho_now, 2.0 * rho_next / half_span))
        rho_now = rho_next
    return 1.0 / middle, updates


def east(x):
    return pltpu.roll(x, x.shape[1] - 1, 1)


def west(x):
    return pltpu.roll(x, 1, 1)


def north(x):
    return pltpu.roll(x, x.shape[0] - 1, 0)


def south(x):
    return pltpu.roll(x, 1, 0)


def slot_lane(field, row):
    return (field % 2) * 64 + row * 8 + (field // 2) * 4


def turn(x, shift):
    shift = shift % LANE
    return x if shift == 0 else pltpu.roll(x, shift, 1)


def kernel(
    levels, total_rows, by_count, bx_count,
    u_in, v_in, t_in, s_in, wind_in, ssh_in, depth_in,
    own, surface_out,
    ext, depth_own, pack_send, pack_recv, far_send, far_recv,
    lap, mix, press, depth_c, depth_e, depth_n, stress, cor,
    flow_sum, moved, moved_rows, moved_cols, moved_corners, flat,
    in_sem, row_send, row_recv, pack_ss, pack_rs, moved_ss, moved_rs,
):
    inputs = (u_in, v_in, t_in, s_in)
    rows = SUB
    span = rows + 2 * HALO
    width = ext.shape[-1]
    cols = width - LANE
    tiles = cols // LANE
    groups = -(-levels // SUB)
    block = SUB * rows
    lead = groups * SUB - levels
    assert lead >= 2
    by = lax.axis_index("by")
    bx = lax.axis_index("bx")

    def device(step_y, step_x):
        return (lax.rem(by + step_y + by_count, by_count), lax.rem(bx + step_x + bx_count, bx_count))

    has_north = by < by_count - 1
    has_south = by > 0

    def where_block(y, action):
        if y == 0:
            action()
        else:
            pl.when(has_north if y > 0 else has_south)(action)

    neighbours = [(y, x) for y in (-1, 0, 1) for x in (-1, 0, 1) if (y, x) != (0, 0)]

    def load_copies(late):
        result = []
        start = BATCH * block if late else lead * rows
        count = (groups - BATCH) * block if late else BATCH * block - lead * rows
        for tile in range(tiles):
            lanes = pl.ds(tile * LANE, LANE)
            for field in range(FIELDS):
                result.append(pltpu.make_async_copy(
                    inputs[field].at[pl.ds(start - lead * rows, count), lanes],
                    own.at[field, tile, pl.ds(start, count)],
                    in_sem.at[tile + tiles * late, field],
                ))
        if late:
            return result
        for tile in range(tiles):
            lanes = pl.ds(tile * LANE, LANE)
            result.append(pltpu.make_async_copy(
                ssh_in.at[:, lanes], own.at[0, tile, pl.ds(rows, rows)], in_sem.at[tile, FIELDS]
            ))
            result.append(pltpu.make_async_copy(
                wind_in.at[:, lanes], own.at[1, tile, pl.ds(0, 2 * rows)], in_sem.at[tile, FIELDS + 1]
            ))
        result.append(pltpu.make_async_copy(depth_in, depth_own, in_sem.at[0, FIELDS + 2]))
        return result

    for copy in load_copies(0) + load_copies(1):
        copy.start()

    barrier = pltpu.get_barrier_semaphore()
    for y in (0, 1, -1):

        def greet(y=y):
            for x in (-1, 0, 1):
                if (y, x) != (0, 0):
                    pl.semaphore_signal(barrier, inc=1, device_id=device(y, x), device_id_type=MESH)

        where_block(y, greet)

    lane = lax.broadcasted_iota(jnp.int32, (SUB, LANE), 1)
    for tile in range(tiles):
        for field in range(2, FIELDS):
            own[field, tile, : lead * rows, :] = jnp.zeros((lead * rows, LANE), jnp.float32)
        if lead > 2:
            for field in range(2):
                own[field, tile, 2 * rows : lead * rows, :] = jnp.zeros(((lead - 2) * rows, LANE), jnp.float32)

    def row_copy(group, side):
        source = HALO + rows - HALO if side == 0 else HALO
        target = 0 if side == 0 else HALO + rows
        return pltpu.make_async_remote_copy(
            src_ref=ext.at[group, :, pl.ds(source, HALO), :, pl.ds(0, cols)],
            dst_ref=ext.at[group, :, pl.ds(target, HALO), :, pl.ds(0, cols)],
            send_sem=row_send.at[side, group],
            recv_sem=row_recv.at[side, group],
            device_id=device(1 - 2 * side, 0),
            device_id_type=MESH,
        )

    def send_all(steps, make):
        for y in (1, -1, 0):

            def act(y=y):
                for step in steps:
                    if step[0] == y:
                        make(step).start()

            where_block(y, act)

    def receive_all(steps, make):
        for y in (0, 1, -1):

            def act(y=y):
                for step in steps:
                    if step[0] == y:
                        make(step).wait_recv()

            where_block(-y, act)

    def sent_all(steps, make):
        for y in (0, 1, -1):

            def act(y=y):
                for step in steps:
                    if step[0] == y:
                        make(step).wait_send()

            where_block(y, act)

    def send_rows(group):
        send_all(lengthways, lambda step: row_copy(group, (1 - step[0]) // 2))

    def receive_rows(group):
        receive_all(lengthways, lambda step: row_copy(group, (1 - step[0]) // 2))

    lengthways = [(1, 0), (-1, 0)]

    batches = ((0, BATCH), (BATCH, groups - BATCH))

    def pack_copy(batch, y, x):
        first, count = batches[batch]
        place = 2 * (y % 3) + (1 - x) // 2
        if y == 0:
            source = pack_send.at[(1 + x) // 2, pl.ds(first, count)]
            target = pack_recv.at[(1 - x) // 2, pl.ds(first, count)]
        else:
            source = far_send.at[(1 - y) // 2, (1 + x) // 2, pl.ds(first // 2, count // 2)]
            target = far_recv.at[(1 - y) // 2, (1 - x) // 2, pl.ds(first // 2, count // 2)]
        return pltpu.make_async_remote_copy(
            src_ref=source,
            dst_ref=target,
            send_sem=pack_ss.at[batch, place],
            recv_sem=pack_rs.at[batch, place],
            device_id=device(y, x),
            device_id_type=MESH,
        )

    sideways = [(y, x) for y in (0, 1, -1) for x in (-1, 1)]

    for copy in load_copies(0):
        copy.wait()
    for tile in range(tiles):
        own[0, tile, :rows, :] = depth_own[:, tile * LANE : (tile + 1) * LANE].astype(jnp.float32)
    pl.semaphore_wait(barrier, 2 + 3 * has_north.astype(jnp.int32) + 3 * has_south.astype(jnp.int32))

    def stage_step(group):
        west_pack = jnp.zeros((SUB, LANE), jnp.float32)
        east_pack = jnp.zeros((SUB, LANE), jnp.float32)
        for field in range(FIELDS):
            for row in range(rows):
                parts = [
                    own[field, tile, pl.ds(group * block + row, SUB, stride=rows), :]
                    for tile in range(tiles)
                ]
                for tile in range(tiles):
                    ext[group, field, HALO + row, :, tile * LANE : (tile + 1) * LANE] = parts[tile]
                first = slot_lane(field, row)
                here = (lane >= first) & (lane < first + HALO)
                west_pack = jnp.where(here, turn(parts[0], first), west_pack)
                east_pack = jnp.where(here, turn(parts[-1], first + HALO), east_pack)
        pack_send[0, group] = west_pack
        pack_send[1, group] = east_pack
        return west_pack, east_pack

    assert groups % BATCH == 0 and BATCH % 2 == 0
    upper = (lane & 32) != 0

    def stage_batch(index, carry):
        for k in range(BATCH // 2):
            pair = index * (BATCH // 2) + k
            packs = stage_step(2 * pair), stage_step(2 * pair + 1)
            for side in range(2):
                far_send[0, side, pair] = jnp.where(upper, packs[0][side], turn(packs[1][side], -32))
                far_send[1, side, pair] = jnp.where(upper, turn(packs[1][side], 32), packs[0][side])

        @pl.when(index == 0)
        def _():
            send_rows(0)
            send_all(sideways, lambda step: pack_copy(0, *step))

            def more(group, inner):
                send_rows(group)
                return inner

            lax.fori_loop(1, BATCH, more, 0)
            for copy in load_copies(1):
                copy.wait()

        return carry

    lax.fori_loop(0, groups // BATCH, stage_batch, 0)
    send_all(sideways, lambda step: pack_copy(1, *step))

    def send_step(group, carry):
        send_rows(group)
        return carry

    lax.fori_loop(BATCH, groups, send_step, 0)

    row_index = by * rows - HALO + lax.broadcasted_iota(jnp.int32, (span, LANE), 0)
    turning = 1.2 * jnp.sin(0.9 * math.pi * ((row_index.astype(jnp.float32) + 0.5) / total_rows - 0.5))
    for row in range(span):
        cor[row] = jnp.broadcast_to(turning[row : row + 1, :], (SUB, LANE))

    sub = lax.broadcasted_iota(jnp.int32, (SUB, width), 0)
    level = sub.astype(jnp.float32)
    zeros = jnp.zeros((SUB, width), jnp.float32)

    for row in range(span):
        press[0, row] = zeros
        press[1, row] = zeros
    for axis in range(2):
        for row in range(rows):
            flow_sum[axis, row] = jnp.zeros((SUB, cols), jnp.float32)

    def operator(field, corner):
        north_field = north(field)
        total = field + north_field
        change = north_field - field
        flux_x = corner * (0.5 * (east(total) - total))
        flux_y = corner * (0.5 * (east(change) + change))
        along_x = flux_x + south(flux_x)
        along_y = flux_y + west(flux_y)
        return PHI * field - 0.5 * ((along_x - west(along_x)) + (along_y - south(along_y)))

    def flat_tables():
        for row in range(span):
            index = by * rows + (row - HALO)
            inside = (index >= 0) & (index < total_rows)
            here = jnp.where(inside, jnp.broadcast_to(ext[0, 0, row, 0:1, :], (SUB, width)), 0.0)
            depth_c[row] = here
            depth_e[row] = jnp.minimum(here, east(here))
            if row > 0:
                depth_n[row - 1] = jnp.minimum(before, here)
            before = here
            for axis in range(2):
                wind = jnp.broadcast_to(ext[0, 1, row, axis : axis + 1, :], (SUB, width))
                stress[axis, row] = jnp.where(sub == lead, WIND * wind, 0.0)
            place = (row + span - HALO) % span
            flat[0, place : place + 1, :] = here[0:1, :]
            flat[1, place : place + 1, :] = jnp.where(inside, ext[0, 0, row, 1:2, :], 0.0)
        depth = flat[0]
        ssh = flat[1]
        near = jnp.minimum(depth, east(depth))
        corner = jnp.minimum(near, north(near)) * (1.0 / levels)
        pair = corner + west(corner)
        ocean = jnp.where(depth > 0.0, 1.0, 0.0)
        flat[2] = corner
        flat[3] = 1.0 / (PHI + 0.5 * (pair + south(pair)))
        flat[4] = ocean
        flat[5] = ocean * (PHI * ssh) - operator(ssh, corner)

    def cut(mask, value):
        return jnp.where(mask, value, 0.0)

    def tendencies(group):
        number = level + (group * SUB - lead).astype(jnp.float32)
        number = jnp.where(number < 0.0, 1e9, number)

        def stage_pass(part):
            slot = group if part == 0 else groups
            keep = width if part == 0 else cols

            def first_block(index, inner):
                row = 1 + 2 * part + index * FIRST
                wet = [number < depth_c[row + k] for k in range(FIRST)]
                wet_e = [number < depth_e[row + k] for k in range(FIRST)]
                wet_n = [number < depth_n[row - 1 + k] for k in range(FIRST + 1)]
                speed = [
                    [(-0.5 * ADVECT) * ext[slot, field, row + k, :, :keep] for field in range(2)] for k in range(FIRST)
                ]
                for field in range(FIELDS):
                    cells = [ext[slot, field, row - 1 + k] for k in range(FIRST + 2)]
                    faces = [cut(wet_n[k], cells[k + 1] - cells[k]) for k in range(FIRST + 1)]
                    for k in range(FIRST):
                        here = cells[k + 1]
                        face_e = cut(wet_e[k], east(here) - here)
                        face_w = west(face_e)
                        lap[field, row + k] = (face_e - face_w) + (faces[k + 1] - faces[k])
                        along_x = (face_e + face_w)[:, :keep]
                        along_y = (faces[k + 1] + faces[k])[:, :keep]
                        mix[field, row + k, :, :keep] = speed[k][0] * along_x + speed[k][1] * along_y
                above = [
                    jnp.broadcast_to(press[part, row + k, SUB - 1 : SUB, :], (SUB, width)) for k in range(FIRST)
                ]
                for k in range(FIRST):
                    running = cut(
                        wet[k],
                        (-0.8 * PRESS) * ext[slot, 2, row + k] + (0.6 * PRESS) * ext[slot, 3, row + k],
                    )
                    for shift in (1, 2, 4):
                        running = running + jnp.where(sub >= shift, pltpu.roll(running, shift, 0), 0.0)
                    press[part, row + k] = above[k] + running
                return inner

            def second_block(index, inner):
                row = 2 + 2 * part + index * SECOND
                wet = [(number < depth_c[row + k])[:, :keep] for k in range(SECOND)]
                wet_e = [number < depth_e[row + k] for k in range(SECOND)]
                wet_n = [(number < depth_n[row - 1 + k])[:, :keep] for k in range(SECOND + 1)]

                def differences(cells):
                    faces = [
                        cut(wet_n[k], cells[k + 1][:, :keep] - cells[k][:, :keep]) for k in range(SECOND + 1)
                    ]
                    result = []
                    for k in range(SECOND):
                        here = cells[k + 1]
                        face_e = cut(wet_e[k], east(here) - here)
                        result.append((face_e[:, :keep], west(face_e)[:, :keep], faces[k + 1], faces[k]))
                    return result

                forced = []
                cells = [press[part, row - 1 + k] for k in range(SECOND + 2)]
                for k, (face_e, face_w, face_n, face_s) in enumerate(differences(cells)):
                    turned = jnp.concatenate([cor[row + k]] * (keep // LANE), axis=1)
                    forced.append((
                        cut(wet[k], turned * ext[slot, 1, row + k, :, :keep]) - 0.5 * (face_e + face_w),
                        cut(wet[k], -turned * ext[slot, 0, row + k, :, :keep]) - 0.5 * (face_n + face_s),
                    ))
                results = []
                for field in range(FIELDS):
                    cells = [lap[field, row - 1 + k] for k in range(SECOND + 2)]
                    for k, (face_e, face_w, face_n, face_s) in enumerate(differences(cells)):
                        twice = (face_e - face_w) + (face_n - face_s)
                        value = (
                            ext[slot, field, row + k, :, :keep] + mix[field, row + k, :, :keep]
                        ) - KAPPA * twice
                        if field < 2:
                            value = value + forced[k][field]
                        if part == 1:
                            value = 0.5 * (ext[group, field, row + k, :, :keep] + value)
                        results.append((field, k, value))
                for field, k, value in results:
                    if part == 0:
                        ext[groups, field, row + k] = value
                        continue
                    inner_row = row + k - HALO
                    for tile in range(tiles):
                        own[field, tile, pl.ds(group * block + inner_row, SUB, stride=rows), :] = value[
                            :, tile * LANE : (tile + 1) * LANE
                        ]
                    if field < 2:
                        flow_sum[field, inner_row] = flow_sum[field, inner_row] + cut(wet[k], value)
                return inner

            lax.fori_loop(0, (span - 2 - 4 * part + FIRST - 1) // FIRST, first_block, 0)
            lax.fori_loop(0, (span - 4 - 4 * part + SECOND - 1) // SECOND, second_block, 0)

            @pl.when(group == 0)
            def _():
                for row in range(2 + 2 * part, span - 2 - 2 * part):
                    for axis in range(2):
                        wind = cut(number < depth_c[row], stress[axis, row])
                        if part == 0:
                            ext[groups, axis, row] = ext[groups, axis, row] + wind
                            continue
                        half = 0.5 * wind[:, :cols]
                        flow_sum[axis, row - HALO] = flow_sum[axis, row - HALO] + half
                        for tile in range(tiles):
                            place = pl.ds(row - HALO, SUB, stride=rows)
                            lanes = slice(tile * LANE, (tile + 1) * LANE)
                            own[axis, tile, place, :] = own[axis, tile, place, :] + half[:, lanes]

        stage_pass(0)
        stage_pass(1)

    west_lanes = (lane & 7) < HALO

    def widen(group):
        pair = lax.div(jnp.int32(group), jnp.int32(2))
        odd = lax.rem(jnp.int32(group), jnp.int32(2))
        packs = [
            [pack_recv[x, group] for x in range(2)],
            [pltpu.roll(far_recv[0, x, pair], 32 * odd, 1) for x in range(2)],
            [pltpu.roll(far_recv[1, x, pair], 96 * odd, 1) for x in range(2)],
        ]
        for field in range(FIELDS):
            shifts = (
                HALO * 8 - slot_lane(field, 0), -slot_lane(field, rows - HALO), (HALO + rows) * 8 - slot_lane(field, 0)
            )
            parts = [
                jnp.where(west_lanes, turn(packs[y][0], shifts[y]), turn(packs[y][1], shifts[y] + HALO))
                for y in range(3)
            ]
            all_rows = jnp.where(
                lane < HALO * 8, parts[1], jnp.where(lane < (HALO + rows) * 8, parts[0], parts[2])
            )
            for row in range(span):
                ext[group, field, row, :, cols:width] = turn(all_rows, LANE - HALO - 8 * row)

    receive_all(sideways, lambda step: pack_copy(0, *step))
    receive_rows(0)
    widen(0)
    flat_tables()

    def group_step(group, carry):
        @pl.when(group == BATCH)
        def _():
            receive_all(sideways, lambda step: pack_copy(1, *step))

        @pl.when(group > 0)
        def _():
            receive_rows(group)
            widen(group)

        tendencies(group)
        return carry

    lax.fori_loop(0, groups, group_step, 0)

    for row in range(rows):
        for axis in range(2):
            total = jnp.sum(flow_sum[axis, row], axis=0, keepdims=True) * (1.0 / levels)
            moved[axis, row : row + 1, :] = total

    def moved_copy(step):
        y, x = step
        place = neighbours.index(step)
        other = neighbours.index((-y, -x))
        if x == 0:
            source, target = moved, moved_rows.at[(1 - y) // 2]
        else:
            tile = tiles - 1 if x > 0 else 0
            source = moved.at[:, :, pl.ds(tile * LANE, LANE)]
            side = (1 - x) // 2
            target = moved_cols.at[side] if y == 0 else moved_corners.at[(1 - y) // 2, side]
        return pltpu.make_async_remote_copy(
            src_ref=source, dst_ref=target, send_sem=moved_ss.at[place], recv_sem=moved_rs.at[place],
            device_id=device(y, x), device_id_type=MESH,
        )

    send_all(neighbours, moved_copy)
    receive_all(neighbours, moved_copy)
    lower = lax.broadcasted_iota(jnp.int32, (SUB, cols), 0) < HALO
    lower_tile = lax.broadcasted_iota(jnp.int32, (SUB, LANE), 0) < HALO
    right = lane < LANE // 2
    def given(side, values):
        return jnp.where(has_north if side == 1 else has_south, values, 0.0)

    transports = []
    for axis in range(2):
        near = jnp.concatenate(
            [moved[axis], jnp.where(right, moved_cols[1, axis], moved_cols[0, axis])], axis=1
        )
        corners = [
            jnp.where(right, moved_corners[side, 1, axis], moved_corners[side, 0, axis]) for side in range(2)
        ]
        far = jnp.concatenate(
            [
                jnp.where(lower, given(1, moved_rows[1, axis]), given(0, moved_rows[0, axis])),
                jnp.where(lower_tile, given(1, corners[1]), given(0, corners[0])),
            ],
            axis=1,
        )
        transports.append(jnp.concatenate([near, far], axis=0))

    corner = flat[2]
    diagonal_inverse = flat[3]
    ocean = flat[4]
    face_x = ocean * east(ocean) * (east(transports[0]) - transports[0])
    face_y = ocean * north(ocean) * (north(transports[1]) - transports[1])
    spread = 0.5 * ((face_x + west(face_x)) + (face_y + south(face_y)))
    residual = flat[5] - (DIVERGE * ocean) * spread
    opening, updates = chebyshev_weights(ITERS)
    direction = opening * (residual * diagonal_inverse)

    def pick(index, values):
        result = jnp.float32(values[-1])
        for k in range(len(values) - 1):
            result = jnp.where(index == k, jnp.float32(values[k]), result)
        return result

    def solve_step(index, carry):
        surface, residual, direction = carry
        surface = surface + direction
        residual = residual - operator(direction, corner)
        keep = pick(index, [item[0] for item in updates])
        push = pick(index, [item[1] for item in updates])
        direction = keep * direction + push * (residual * diagonal_inverse)
        return surface, residual, direction

    surface, residual, direction = lax.fori_loop(0, ITERS - 1, solve_step, (flat[1], residual, direction))
    surface_out[...] = (surface + direction)[:rows, :cols]

    sent_all(neighbours, moved_copy)
    for batch in range(2):
        sent_all(sideways, lambda step: pack_copy(batch, *step))

    def drain(group, carry):
        sent_all(lengthways, lambda step: row_copy(group, (1 - step[0]) // 2))
        return carry

    lax.fori_loop(0, groups, drain, 0)


def deliver(lead, fields_in, surface_in, u_out, v_out, t_out, s_out, surface_out, sems):
    outputs = (u_out, v_out, t_out, s_out)
    count = u_out.shape[0]
    copies = [
        pltpu.make_async_copy(
            fields_in.at[field, tile, pl.ds(lead, count)],
            outputs[field].at[:, pl.ds(tile * LANE, LANE)],
            sems.at[field, tile],
        )
        for field in range(FIELDS)
        for tile in range(fields_in.shape[1])
    ]
    copies.append(pltpu.make_async_copy(surface_in, surface_out, sems.at[FIELDS, 0]))
    for copy in copies:
        copy.start()
    for copy in copies:
        copy.wait()


def body(by_count, bx_count, u, v, t, s, wind, ssh, depth):
    levels, rows, cols = u.shape
    groups = -(-levels // SUB)
    span = rows + 2 * HALO
    room = span + 4
    tiles = cols // LANE
    width = cols + LANE
    f32 = jnp.float32
    flat_shape = (levels * rows, cols)
    args = [item.reshape(flat_shape) for item in (u, v, t, s)]
    own = jax.ShapeDtypeStruct((FIELDS, tiles, (groups + 1) * SUB * rows, LANE), f32)
    done, surface = pl.pallas_call(
        functools.partial(kernel, levels, rows * by_count, by_count, bx_count),
        out_shape=[pltpu.VMEM(own.shape, f32), pltpu.VMEM(ssh.shape, f32)],
        in_specs=[pl.BlockSpec(memory_space=pltpu.HBM)] * (FIELDS + 3),
        out_specs=[pl.BlockSpec(memory_space=pltpu.VMEM)] * 2,
        scratch_shapes=[
            pltpu.VMEM((groups + 1, FIELDS, room, SUB, width), f32),
            pltpu.VMEM((rows, cols), jnp.int32),
            pltpu.VMEM((2, groups, SUB, LANE), f32),
            pltpu.VMEM((2, groups, SUB, LANE), f32),
            pltpu.VMEM((2, 2, groups // 2, SUB, LANE), f32),
            pltpu.VMEM((2, 2, groups // 2, SUB, LANE), f32),
            pltpu.VMEM((FIELDS, room, SUB, width), f32),
            pltpu.VMEM((FIELDS, room, SUB, width), f32),
            pltpu.VMEM((2, room, SUB, width), f32),
            pltpu.VMEM((room, SUB, width), f32),
            pltpu.VMEM((room, SUB, width), f32),
            pltpu.VMEM((room, SUB, width), f32),
            pltpu.VMEM((2, room, SUB, width), f32),
            pltpu.VMEM((room, SUB, LANE), f32),
            pltpu.VMEM((2, rows, SUB, cols), f32),
            pltpu.VMEM((2, rows, cols), f32),
            pltpu.VMEM((2, 2, rows, cols), f32),
            pltpu.VMEM((2, 2, rows, LANE), f32),
            pltpu.VMEM((2, 2, 2, rows, LANE), f32),
            pltpu.VMEM((6, span, width), f32),
            pltpu.SemaphoreType.DMA((2 * tiles, FIELDS + 3)),
            pltpu.SemaphoreType.DMA((2, groups)),
            pltpu.SemaphoreType.DMA((2, groups)),
            pltpu.SemaphoreType.DMA((2, 6)),
            pltpu.SemaphoreType.DMA((2, 6)),
            pltpu.SemaphoreType.DMA((8,)),
            pltpu.SemaphoreType.DMA((8,)),
        ],
        compiler_params=pltpu.CompilerParams(
            collective_id=0, has_side_effects=True, vmem_limit_bytes=61 << 20
        ),
    )(*args, wind.reshape(2 * rows, cols), ssh, depth)
    outs = pl.pallas_call(
        functools.partial(deliver, (groups * SUB - levels) * rows),
        out_shape=[jax.ShapeDtypeStruct(flat_shape, f32)] * FIELDS + [jax.ShapeDtypeStruct(ssh.shape, f32)],
        in_specs=[pl.BlockSpec(memory_space=pltpu.VMEM)] * 2,
        out_specs=[pl.BlockSpec(memory_space=pltpu.HBM)] * (FIELDS + 1),
        scratch_shapes=[pltpu.SemaphoreType.DMA((FIELDS + 1, tiles))],
        compiler_params=pltpu.CompilerParams(vmem_limit_bytes=4 << 20),
    )(done, surface)
    return tuple(item.reshape(u.shape) for item in outs[:FIELDS]) + (outs[FIELDS],)


def solution(mesh):
    whole = P(None, "by", "bx")
    flat = P("by", "bx")
    return jax.shard_map(
        functools.partial(body, mesh.shape["by"], mesh.shape["bx"]),
        mesh=mesh,
        in_specs=(whole,) * 5 + (flat, flat),
        out_specs=(whole,) * 4 + (flat,),
        check_vma=False,
    )
```
